512 devices in a mesh: prow: 16 (over y, x), pcol: 32 (over z, core).
Axes of the slice: x: 4, y: 4, z: 16, core: 2. Of those that a mesh axis runs over, the one named last changes fastest.
Arguments:
- matrix: float32 [4, 16, 256, 2, 32, 256], P(None, 'prow', None, None, 'pcol'), may hold values from -6 to 6
- pivots: int32 [2, 256], replicated, may hold values from 256 to 16383, as said below
- inverse_blocks: float32 [2, 256, 256], replicated, may hold values from -1 to 1
Outputs:
- factored: float32 [4, 16, 256, 2, 32, 256], P(None, 'prow', None, None, 'pcol')
The draws below stay inside these ranges and needn't reach their ends.
Inputs may be any that keep to these rules, and one draw needn't show every extreme that they name: Entries of pivots[0] lie in 256 to 16383, entries of pivots[1] in 512 to 16383; the entries of one panel are distinct.
All inputs are finite; a program needn't handle non-finite values.
Results may differ from the reference program's by a relative error of at most 0.00013.
Values sent between devices are 32-bit elements; how exact they have to be, the bound alone decides.
A program may use at most 64 MiB of HBM per device.

```python
import jax
import jax.numpy as jnp
from jax import lax

N = 16384
NB = 256
RBD = 4
CBD = 2
N_PROW = 16
N_PCOL = 32


def draw_pivots(key, part):
    key = jax.random.fold_in(key, 5)
    panels = []
    for section in range(2):
        lowest = (section + 1) * NB
        sub_key = jax.random.fold_in(key, section)
        shuffled = jax.random.permutation(sub_key, N - lowest - 2).astype(jnp.int32) + lowest + 1
        listed = jnp.concatenate([jnp.array([lowest], jnp.int32), shuffled[:NB - 2], jnp.array([N - 1], jnp.int32)])
        order_key = jax.random.fold_in(sub_key, 7)
        panels.append(jax.random.permutation(order_key, listed))
    return jnp.stack(panels).astype(jnp.int32)


def draw_inverse_blocks(key, part):
    key = jax.random.fold_in(key, 9)
    noise_key, diag_key = jax.random.split(key)
    noise = jax.random.normal(noise_key, (2, NB, NB), jnp.float32)
    offdiag = jnp.clip(noise / jnp.sqrt(jnp.float32(NB)), -1.0, 1.0)
    diag_vals = jax.random.uniform(diag_key, (2, NB), jnp.float32, 0.7, 1.3)
    scale = 1.0 / jnp.sqrt(jnp.float32(NB))
    rows = jnp.arange(NB)[:, None]
    cols = jnp.arange(NB)[None, :]
    upper_part = jnp.where(cols > rows, offdiag * scale, 0.0)
    diag_part = jnp.where(cols == rows, diag_vals[:, :, None] * scale, 0.0)
    lower_part = jnp.where(cols < rows, offdiag, 0.0)
    return (upper_part + diag_part + lower_part).astype(jnp.float32)


def block_scale(stream_key, extent, shards, low, high):
    gain = 1.0
    for dim, parts in shards:
        heights = jax.random.uniform(jax.random.fold_in(jax.random.fold_in(stream_key, 6), dim), (parts,), jnp.float32, low / len(shards), high / len(shards))
        gain = gain * jnp.repeat(jnp.exp(heights), extent[dim] // parts).reshape((-1,) + (1,) * (len(extent) - 1 - dim))
    return gain


def centred(key, dims, scale, reach, cuts=(), held_as=jnp.bfloat16):
    entries = jax.random.normal(key, dims, jnp.float32) * scale
    if len(cuts) > 0:
        entries = block_scale(key, dims, cuts, -0.22, 0.18) * entries
    return jnp.clip(entries, min=-reach, max=reach).astype(held_as)


def setup_inputs(seed: int = 0) -> dict:
    arg_keys = jax.random.split(jax.random.key(seed), 4)
    return {
        "matrix": centred(arg_keys[0], (RBD, N_PROW, NB, CBD, N_PCOL, NB), 1.0, 6.0, ((1, 16), (4, 32)), jnp.float32),
        "pivots": draw_pivots(jax.random.fold_in(arg_keys[3], 71), 0),
        "inverse_blocks": draw_inverse_blocks(jax.random.fold_in(arg_keys[3], 71), 0),
    }


def reference(matrix, pivots, inverse_blocks):
    matrix_now = matrix.reshape(N, N)
    identity = jnp.eye(NB, dtype=jnp.float32)
    for section in range(2):
        row_top = section * NB
        row_mid = row_top + NB
        pivot_list = pivots[section]
        block_rows = matrix_now[row_top:row_mid]
        chosen = matrix_now[pivot_list]
        matrix_now = matrix_now.at[row_top:row_mid].set(chosen).at[pivot_list].set(block_rows)
        packed = inverse_blocks[section]
        upper_inv = jnp.triu(packed)
        lower_inv = jnp.tril(packed, -1) + identity
        lower_panel = jnp.dot(matrix_now[row_mid:, row_top:row_mid], upper_inv, precision=lax.Precision.HIGHEST, preferred_element_type=jnp.float32)
        upper_rows = jnp.dot(lower_inv, matrix_now[row_top:row_mid, row_mid:], precision=lax.Precision.HIGHEST, preferred_element_type=jnp.float32)
        matrix_now = matrix_now.at[row_mid:, row_top:row_mid].set(lower_panel)
        matrix_now = matrix_now.at[row_top:row_mid, row_mid:].set(upper_rows)
        update = jnp.dot(lower_panel, upper_rows, precision=lax.Precision.HIGHEST, preferred_element_type=jnp.float32)
        matrix_now = matrix_now.at[row_mid:, row_mid:].add(-update)
    return matrix_now.reshape(matrix.shape)
```

```python
import functools

import jax
import jax.numpy as jnp
from jax import lax
from jax.experimental import pallas as pl
from jax.experimental.pallas import tpu as pltpu
from jax.sharding import PartitionSpec as P

F32, BF16 = jnp.float32, jnp.bfloat16
CHUNKS = 20


def mul(left, right):
    return jnp.dot(left, right, preferred_element_type=F32)


def parts2(x):
    high = x.astype(BF16)
    return high, (x - high.astype(F32)).astype(BF16)


def parts3(x):
    high = x.astype(BF16)
    rest = x - high.astype(F32)
    mid = rest.astype(BF16)
    return high, mid, (rest - mid.astype(F32)).astype(BF16)


def product(left, right):
    lh, ll = parts2(left)
    rh, rl = parts2(right)
    return mul(lh, rh) + (mul(lh, rl) + mul(ll, rh))


def kernel(
    sizes, x, piv, pivt, inv, out,
    a, s0, s1, s2, picks, rs, ag, panel, u, uh, ul, old0, old1, old2,
    in_sem, out_sem, rs_send, rs_recv, old_send, old_recv, ag_send, ag_recv,
    z_send, z_send2, z_recv, sib_send, sib_recv,
):
    rb, cb, nb, np_, nz = sizes
    rows, width, slots = rb * nb, cb * nb, 2 * nb
    ch, co = slots // np_, nb // np_
    height = nb + rows
    piece = height // CHUNKS
    me = lax.axis_index("prow")
    col = lax.axis_index("pcol")
    z, core = col // 2, col % 2

    def at_row(r):
        return {"prow": r, "pcol": col}

    def at_col(zz, cc):
        return {"prow": me, "pcol": zz * 2 + cc}

    def load(r, c):
        return pltpu.make_async_copy(
            x.at[r, 0, :, c, 0, :],
            a.at[pl.ds(r * nb, nb), pl.ds(c * nb, nb)],
            in_sem.at[r * cb + c],
        )

    for r in range(rb):
        for c in range(cb):
            load(r, c).start()

    barrier = pltpu.get_barrier_semaphore()

    def greet(d, carry):
        pl.semaphore_signal(barrier, inc=1, device_id=at_row((me + d) % np_))
        return carry

    lax.fori_loop(1, np_, greet, 0)
    for zz, cc in (((z + 1) % nz, core), ((z + nz - 1) % nz, core), (z, 1 - core)):
        pl.semaphore_signal(barrier, inc=1, device_id=at_col(zz, cc))

    p0r, p1r = piv[0:1, :], piv[1:2, :]
    p0c, p1c = pivt[:, 0:1], pivt[:, 1:2]
    lane = lax.broadcasted_iota(jnp.int32, (nb, nb), 1)
    sub = lax.broadcasted_iota(jnp.int32, (nb, nb), 0)
    same = p1c == p0r
    back = jnp.max(jnp.where(same, lane, -1), axis=1, keepdims=True)
    src0, src1 = p0c, jnp.where(back >= 0, back, p1c)
    hit = jnp.max(jnp.where(p0r == sub + nb, p1c, -1), axis=0, keepdims=True)
    gone = jnp.max(jnp.where(same, 1, 0), axis=0, keepdims=True)
    dst0 = jnp.where(hit >= 0, hit, jnp.where(gone > 0, -1, p0r))
    up = jnp.max(jnp.where(p0c == lane + nb, 1, 0), axis=0, keepdims=True)
    dst1 = jnp.where(up > 0, -1, p1r)

    for r in range(rb):
        for c in range(cb):
            load(r, c).wait()

    def split(r, carry):
        at = pl.ds(pl.multiple_of(r * nb, nb), nb)
        h, m, l = parts3(a[at, :])
        s0[at, :], s1[at, :], s2[at, :] = h, m, l
        return carry

    lax.fori_loop(0, rb, split, 0)
    for k, src in ((0, src0), (1, src1)):
        total = jnp.zeros((nb, width), F32)
        for r in range(rb):
            here = (r * np_ + me) * nb + lane
            pick = (src == here).astype(F32).astype(BF16)
            at = pl.ds(r * nb, nb)
            total = total + (mul(pick, s0[at, :]) + mul(pick, s1[at, :]) + mul(pick, s2[at, :]))
        picks[pl.ds(k * nb, nb), :] = total

    pl.semaphore_wait(barrier, np_ - 1 + 3)

    def rs_copy(d):
        to = (me + d) % np_
        return pltpu.make_async_remote_copy(
            picks.at[pl.ds(pl.multiple_of(to * ch, ch), ch), :], rs.at[me],
            rs_send.at[d], rs_recv.at[d], device_id=at_row(to),
        )

    def old_copy(k, d):
        to = (me + d) % np_
        return pltpu.make_async_remote_copy(
            a.at[pl.ds(pl.multiple_of(to * co, co), co), :],
            ag.at[to, pl.ds(ch + k * co, co), :],
            old_send.at[d], old_recv.at[k], device_id=at_row(to),
        )

    def ag_copy(d):
        return pltpu.make_async_remote_copy(
            ag.at[me], ag.at[me], ag_send.at[d], ag_recv.at[d], device_id=at_row((me + d) % np_),
        )

    def loop(low, high, body):
        def step(d, carry):
            body(d)
            return carry

        lax.fori_loop(low, high, step, 0)

    for k in range(2):
        @pl.when(me == k)
        def _():
            loop(1, np_, lambda d: old_copy(k, d).start())
            ag[me, pl.ds(ch + k * co, co), :] = a[pl.ds(pl.multiple_of(me * co, co), co), :]

    loop(1, np_, lambda d: rs_copy(d).start())
    ag[me, pl.ds(0, ch), :] = picks[pl.ds(pl.multiple_of(me * ch, ch), ch), :]

    def add(d):
        pltpu.make_async_remote_copy(
            rs.at[me], rs.at[(me + np_ - d) % np_], rs_send.at[d], rs_recv.at[d], device_id=at_row((me + d) % np_),
        ).wait_recv()
        ag[me, pl.ds(0, ch), :] = ag[me, pl.ds(0, ch), :] + rs[(me + np_ - d) % np_]

    loop(1, np_, add)
    for k in range(2):
        @pl.when(me != k)
        def _():
            pltpu.make_async_remote_copy(
                ag.at[me, pl.ds(ch, co), :], ag.at[me, pl.ds(ch + k * co, co), :],
                old_send.at[0], old_recv.at[k], device_id=at_row((me + 1) % np_),
            ).wait_recv()

    loop(1, np_, lambda d: ag_copy(d).start())

    def ag_wait(d):
        pltpu.make_async_remote_copy(
            ag.at[me], ag.at[(me + np_ - d) % np_], ag_send.at[d], ag_recv.at[d], device_id=at_row((me + d) % np_),
        ).wait_recv()

    loop(1, np_, ag_wait)
    for k in range(2):
        @pl.when(me == k)
        def _():
            loop(1, np_, lambda d: old_copy(k, d).wait_send())

    for k in range(2):
        at = pl.ds(k * nb, nb)
        h, m, l = parts3(ag[:, pl.ds(ch + k * co, co), :].reshape(nb, width))
        old0[at, :], old1[at, :], old2[at, :] = h, m, l

    def place(c):
        cs = pl.ds(c * nb, nb)

        def step(r):
            at = pl.ds(pl.multiple_of(r * nb, nb), nb)
            here = (r * np_ + me) * nb + sub
            total, moved = jnp.zeros((nb, nb), F32), jnp.zeros((nb, 1), F32)
            for k, dst in ((0, dst0), (1, dst1)):
                put = (dst == here).astype(F32)
                moved = jnp.maximum(moved, jnp.max(put, axis=1, keepdims=True))
                put = put.astype(BF16)
                ks = pl.ds(k * nb, nb)
                total = total + (mul(put, old0[ks, cs]) + mul(put, old1[ks, cs]) + mul(put, old2[ks, cs]))
            a[at, cs] = jnp.where(moved > 0, total, a[at, cs])

        loop(0, rb, step)
        for k in range(2):
            @pl.when(me == k)
            def _():
                half = np_ // 2
                a[pl.ds(0, nb), cs] = ag[pl.ds(k * half, half), pl.ds(0, ch), cs].reshape(nb, nb)

    def z_copy(i, zz, sem):
        at = panel.at[core, pl.ds(pl.multiple_of(i * piece, piece), piece), :]
        return pltpu.make_async_remote_copy(at, at, sem.at[i], z_recv.at[i], device_id=at_col(zz, core))

    def sib_copy(i):
        at = panel.at[core, pl.ds(pl.multiple_of(i * piece, piece), piece), :]
        return pltpu.make_async_remote_copy(at, at, sib_send.at[i], sib_recv.at[i], device_id=at_col(z, 1 - core))

    def sib_wait(i):
        at = panel.at[1 - core, pl.ds(pl.multiple_of(i * piece, piece), piece), :]
        pltpu.make_async_remote_copy(at, at, sib_send.at[i], sib_recv.at[i], device_id=at_col(z, 1 - core)).wait_recv()

    middle = nz // 2
    place(0)

    @pl.when(z == 0)
    def _():
        half = np_ // 2
        for k in range(2):
            @pl.when(core == k)
            def _():
                panel[core, pl.ds(0, nb), :] = ag[pl.ds((1 - k) * half, half), pl.ds(0, ch), pl.ds(0, nb)].reshape(nb, nb)
        panel[core, pl.ds(nb, rows), :] = a[:, pl.ds(0, nb)]

        def send(i):
            z_copy(i, 1, z_send).start()
            z_copy(i, nz - 1, z_send2).start()
            sib_copy(i).start()

        loop(0, CHUNKS, send)

    for c in range(1, cb):
        place(c)

    @pl.when(z != 0)
    def _():
        def relay(i):
            z_copy(i, z, z_send).wait_recv()

            @pl.when(jnp.logical_and(z < middle, z > 0))
            def _():
                z_copy(i, z + 1, z_send).start()

            @pl.when(z > middle + 1)
            def _():
                z_copy(i, z - 1, z_send).start()

            sib_copy(i).start()

        loop(0, CHUNKS, relay)

    ui0 = jnp.where(lane >= sub, inv[0], 0.0)
    ui1 = jnp.where(lane >= sub, inv[1], 0.0)
    eye = jnp.where(lane == sub, 1.0, 0.0)
    li0 = jnp.where(lane < sub, inv[0], 0.0) + eye
    li1 = jnp.where(lane < sub, inv[1], 0.0) + eye
    half = np_ // 2
    pr0 = ag[pl.ds(0, half), pl.ds(0, ch), :].reshape(nb, width)
    pr1 = ag[pl.ds(half, half), pl.ds(0, ch), :].reshape(nb, width)
    wide = lax.broadcasted_iota(jnp.int32, (nb, width), 1)
    block = jnp.where(wide < nb, col, 2 * nz)
    u0 = jnp.where(block > 0, product(li0, pr0), 0.0)

    loop(0, CHUNKS, sib_wait)
    l10 = product(panel[0, pl.ds(0, nb), :], ui0)
    u01 = product(li0, panel[1, pl.ds(0, nb), :])
    u1 = jnp.where(block > 1, product(li1, pr1 - product(l10, u0)), 0.0)
    u[pl.ds(0, nb), :], u[pl.ds(nb, nb), :] = u0, u1
    uh[pl.ds(0, nb), :], ul[pl.ds(0, nb), :] = parts2(u0)
    uh[pl.ds(nb, nb), :], ul[pl.ds(nb, nb), :] = parts2(u1)

    def store(r, c):
        return pltpu.make_async_copy(
            a.at[pl.ds(r * nb, nb), pl.ds(c * nb, nb)],
            out.at[r, 0, :, c, 0, :],
            out_sem.at[r * cb + c],
        )

    def update(r):
        at = pl.ds(pl.multiple_of(r * nb, nb), nb)
        below = pl.ds(pl.multiple_of(nb + r * nb, nb), nb)
        part = r * np_ + me
        l0 = jnp.where(part > 0, product(panel[0, below, :], ui0), 0.0)
        l1 = product(panel[1, below, :] - product(l0, u01), ui1)
        l1 = jnp.where(part > 1, l1, 0.0)
        total = a[at, :]
        for k, l in ((0, l0), (1, l1)):
            ks = pl.ds(k * nb, nb)
            h, m = parts2(l)
            total = total - (mul(h, uh[ks, :]) + (mul(h, ul[ks, :]) + mul(m, uh[ks, :])))
        new = jnp.where(jnp.logical_and(part == 0, block > 0), u[pl.ds(0, nb), :], total)
        new = jnp.where(jnp.logical_and(part == 1, block > 1), u[pl.ds(nb, nb), :], new)
        a[at, :] = new

        @pl.when(jnp.logical_and(col == 0, part > 0))
        def _():
            a[at, pl.ds(0, nb)] = l0

        @pl.when(jnp.logical_and(col == 1, part > 1))
        def _():
            a[at, pl.ds(0, nb)] = l1

    for r in range(rb):
        update(r)
        for c in range(cb):
            store(r, c).start()

    loop(1, np_, lambda d: rs_copy(d).wait_send())
    loop(1, np_, lambda d: ag_copy(d).wait_send())
    loop(0, CHUNKS, lambda i: sib_copy(i).wait_send())

    @pl.when(jnp.logical_or(z < middle, z > middle + 1))
    def _():
        loop(0, CHUNKS, lambda i: z_copy(i, z, z_send).wait_send())

    @pl.when(z == 0)
    def _():
        loop(0, CHUNKS, lambda i: z_copy(i, z, z_send2).wait_send())

    for r in range(rb):
        for c in range(cb):
            store(r, c).wait()


def shards(proc_rows, proc_cols, matrix, pivots, inverse_blocks):
    rb, _, nb, cb, _, _ = matrix.shape
    nz = proc_cols // 2
    rows, width, slots = rb * nb, cb * nb, 2 * nb
    ch, co = slots // proc_rows, nb // proc_rows
    dma = pltpu.SemaphoreType.DMA
    vmem = pl.BlockSpec(memory_space=pltpu.VMEM)
    return pl.pallas_call(
        functools.partial(kernel, (rb, cb, nb, proc_rows, nz)),
        out_shape=jax.ShapeDtypeStruct(matrix.shape, F32),
        in_specs=[pl.BlockSpec(memory_space=pl.ANY), vmem, vmem, vmem],
        out_specs=pl.BlockSpec(memory_space=pl.ANY),
        scratch_shapes=[
            pltpu.VMEM((rows, width), F32),
            pltpu.VMEM((rows, width), BF16),
            pltpu.VMEM((rows, width), BF16),
            pltpu.VMEM((rows, width), BF16),
            pltpu.VMEM((slots, width), F32),
            pltpu.VMEM((proc_rows, ch, width), F32),
            pltpu.VMEM((proc_rows, ch + 2 * co, width), F32),
            pltpu.VMEM((2, nb + rows, nb), F32),
            pltpu.VMEM((slots, width), F32),
            pltpu.VMEM((slots, width), BF16),
            pltpu.VMEM((slots, width), BF16),
            pltpu.VMEM((slots, width), BF16),
            pltpu.VMEM((slots, width), BF16),
            pltpu.VMEM((slots, width), BF16),
            dma((rb * cb,)), dma((rb * cb,)),
            dma((proc_rows,)), dma((proc_rows,)),
            dma((proc_rows,)), dma((2,)),
            dma((proc_rows,)), dma((proc_rows,)),
            dma((CHUNKS,)), dma((CHUNKS,)), dma((CHUNKS,)),
            dma((CHUNKS,)), dma((CHUNKS,)),
        ],
        compiler_params=pltpu.CompilerParams(
            collective_id=0, has_side_effects=True, vmem_limit_bytes=48 * 2**20
        ),
    )(matrix, pivots, pivots.T, inverse_blocks)


def solution(mesh):
    spec = P(None, "prow", None, None, "pcol", None)
    return jax.shard_map(
        functools.partial(shards, mesh.shape["prow"], mesh.shape["pcol"]),
        mesh=mesh,
        in_specs=(spec, P(), P()),
        out_specs=spec,
        check_vma=False,
    )
```

```python
import functools

import jax
import jax.numpy as jnp
from jax import lax
from jax.experimental import pallas as pl
from jax.experimental.pallas import tpu as pltpu
from jax.sharding import PartitionSpec as P

F32, BF16 = jnp.float32, jnp.bfloat16
PIECE_OF_BLOCK = 8
EXTRA = 11


def mul(left, right):
    return jnp.dot(left, right, preferred_element_type=F32)


def parts2(x):
    high = x.astype(BF16)
    return high, (x - high.astype(F32)).astype(BF16)


def parts3(x):
    high = x.astype(BF16)
    rest = x - high.astype(F32)
    mid = rest.astype(BF16)
    return high, mid, (rest - mid.astype(F32)).astype(BF16)


def across(*x):
    return jnp.concatenate(x, axis=1)


def down(*x):
    return jnp.concatenate(x, axis=0)


def weights(x):
    high, low = parts2(x)
    return down(high, low, high)


def product(left, right):
    high, low = parts2(left)
    return mul(across(high, high, low), weights(right))


def kernel(
    sizes, x, piv_in, inv_in, out,
    piv, inv, a, split, picks, rs, aold, apr, panel, corner, u, w0, w1, wu, old,
    in_sem, out_sem, rs_send, rs_recv, old_send, old_recv, aold_send, aold_recv, apr_send, apr_recv,
    z_send, z_send2, z_recv, sib_send, sib_recv,
):
    rb, cb, nb, np_, nz = sizes
    rows, slots = rb * nb, 2 * nb
    ch, co = slots // np_, nb // np_
    half = np_ // 2
    piece = nb // PIECE_OF_BLOCK
    chunks = (rb + 1) * PIECE_OF_BLOCK
    early = (rb - 1) * PIECE_OF_BLOCK
    me = lax.axis_index("prow")
    col = lax.axis_index("pcol")
    z, core = col // 2, col % 2
    middle = nz // 2

    def at_row(r):
        return {"prow": r, "pcol": col}

    def at_col(zz, cc):
        return {"prow": me, "pcol": zz * 2 + cc}

    def loop(low, high, body):
        def step(d, carry):
            body(d)
            return carry

        lax.fori_loop(low, high, step, 0)

    def load(r, c):
        return pltpu.make_async_copy(
            x.at[r, 0, :, c, 0, :], a.at[c, pl.ds(r * nb, nb), :], in_sem.at[r * cb + c]
        )

    load_piv = pltpu.make_async_copy(piv_in, piv, in_sem.at[rb * cb])
    load_inv = pltpu.make_async_copy(inv_in, inv, in_sem.at[rb * cb + 1])
    load_piv.start()
    for c in range(cb):
        for r in range(rb):
            load(r, c).start()
    load_inv.start()

    barrier = pltpu.get_barrier_semaphore()
    loop(1, np_, lambda d: pl.semaphore_signal(barrier, inc=1, device_id=at_row((me + d) % np_)))
    for zz, cc in (((z + 1) % nz, core), ((z + nz - 1) % nz, core), (z, 1 - core)):
        pl.semaphore_signal(barrier, inc=1, device_id=at_col(zz, cc))

    load_piv.wait()
    lane = lax.broadcasted_iota(jnp.int32, (nb, nb), 1)
    sub = lax.broadcasted_iota(jnp.int32, (nb, nb), 0)
    p0r, p1r = piv[0:1, :], piv[1:2, :]
    p0c = jnp.max(jnp.where(lane == sub, p0r, -1), axis=1, keepdims=True)
    p1c = jnp.max(jnp.where(lane == sub, p1r, -1), axis=1, keepdims=True)
    same = p1c == p0r
    back = jnp.max(jnp.where(same, lane, -1), axis=1, keepdims=True)
    src0, src1 = p0c, jnp.where(back >= 0, back, p1c)
    hit = jnp.max(jnp.where(p0r == sub + nb, p1c, -1), axis=0, keepdims=True)
    gone = jnp.max(jnp.where(same, 1, 0), axis=0, keepdims=True)
    dst0 = jnp.where(hit >= 0, hit, jnp.where(gone > 0, -1, p0r))
    up = jnp.max(jnp.where(p0c == lane + nb, 1, 0), axis=0, keepdims=True)
    dst1 = jnp.where(up > 0, -1, p1r)

    def old_copy(c, k, d):
        to = (me + d) % np_
        return pltpu.make_async_remote_copy(
            a.at[c, pl.ds(pl.multiple_of(to * co, co), co), :],
            aold.at[c, to, pl.ds(k * co, co), :],
            old_send.at[c], old_recv.at[c, k], device_id=at_row(to),
        )

    def old_scatter(c):
        for k in range(2):
            @pl.when(me == k)
            def _():
                loop(1, np_, lambda d: old_copy(c, k, d).start())
                aold[c, me, pl.ds(k * co, co), :] = a[c, pl.ds(pl.multiple_of(me * co, co), co), :]

    def old_ready(c):
        for k in range(2):
            @pl.when(me != k)
            def _():
                pltpu.make_async_remote_copy(
                    aold.at[c, me, pl.ds(k * co, co), :], aold.at[c, me, pl.ds(k * co, co), :],
                    old_send.at[c], old_recv.at[c, k], device_id=at_row((me + 1) % np_),
                ).wait_recv()

    def old_drain(c):
        for k in range(2):
            @pl.when(me == k)
            def _():
                sent = a.at[c, pl.ds(0, nb - co), :]
                pltpu.make_async_remote_copy(
                    sent, sent, old_send.at[c], old_recv.at[c, k], device_id=at_row((me + 1) % np_)
                ).wait_send()

    def gather(buf, send, recv, c):
        def start(d):
            pltpu.make_async_remote_copy(
                buf.at[c, me], buf.at[c, me], send.at[c], recv.at[c], device_id=at_row((me + d) % np_)
            ).start()

        loop(1, np_, start)

    def peers(buf, send, recv, c):
        others = buf.at[c, pl.ds(0, np_ - 1)]
        return pltpu.make_async_remote_copy(
            others, others, send.at[c], recv.at[c], device_id=at_row((me + 1) % np_)
        )

    def gather_wait(*which):
        peers(*which).wait_recv()

    old_g, pr_g = (aold, aold_send, aold_recv), (apr, apr_send, apr_recv)

    def pick(c):
        def step(r):
            h, m, l = parts3(a[c, pl.ds(pl.multiple_of(r * nb, nb), nb), :])
            split[0, pl.ds(pl.multiple_of(r * nb, nb), nb), :] = h
            split[1, pl.ds(pl.multiple_of(r * nb, nb), nb), :] = m
            split[2, pl.ds(pl.multiple_of(r * nb, nb), nb), :] = l

        loop(0, rb, step)
        for k, src in ((0, src0), (1, src1)):
            chosen = across(*[(src == (r * np_ + me) * nb + lane).astype(F32).astype(BF16) for r in range(rb)])
            picks[c, pl.ds(k * nb, nb), :] = mul(chosen, split[0]) + mul(chosen, split[1]) + mul(chosen, split[2])

    def rs_start(c):
        rs[c, me] = picks[c, pl.ds(pl.multiple_of(me * ch, ch), ch), :]

        def start(d):
            to = (me + d) % np_
            pltpu.make_async_remote_copy(
                picks.at[c, pl.ds(pl.multiple_of(to * ch, ch), ch), :], rs.at[c, me],
                rs_send.at[c], rs_recv.at[c], device_id=at_row(to),
            ).start()

        loop(1, np_, start)

    def rs_finish(c):
        peers(rs, rs_send, rs_recv, c).wait_recv()
        apr[c, me] = jnp.sum(rs[c], axis=0)

    def old_parts(c):
        for k in range(2):
            at = pl.ds(k * nb, nb)
            old[0, at, :], old[1, at, :], old[2, at, :] = parts3(aold[c, :, pl.ds(k * co, co), :].reshape(nb, nb))

    def place(c, r):
        at = pl.ds(r * nb, nb)
        here = (r * np_ + me) * nb + sub
        put0, put1 = (dst0 == here).astype(F32), (dst1 == here).astype(F32)
        moved = jnp.max(jnp.maximum(put0, put1), axis=1, keepdims=True)
        put = across(put0.astype(BF16), put1.astype(BF16))
        total = mul(put, old[0]) + mul(put, old[1]) + mul(put, old[2])
        a[c, at, :] = jnp.where(moved > 0, total, a[c, at, :])

    def piece_at(i, which):
        return panel.at[which, pl.ds(pl.multiple_of(i * piece, piece), piece), :]

    def z_copy(i, zz, sem):
        at = piece_at(i, core)
        return pltpu.make_async_remote_copy(at, at, sem, z_recv.at[i], device_id=at_col(zz, core))

    def sib_copy(i):
        at = piece_at(i, core)
        return pltpu.make_async_remote_copy(
            at, at, sib_send, sib_recv.at[i // PIECE_OF_BLOCK], device_id=at_col(z, 1 - core)
        )

    def sib_wait(t):
        at = panel.at[1 - core, pl.ds(t * nb, nb), :]
        pltpu.make_async_remote_copy(at, at, sib_send, sib_recv.at[t], device_id=at_col(z, 1 - core)).wait_recv()

    def send(i):
        z_copy(i, 1, z_send).start()
        z_copy(i, nz - 1, z_send2).start()
        sib_copy(i).start()

    def relay(i):
        z_copy(i, z, z_send).wait_recv()

        @pl.when(jnp.logical_and(z < middle, z > 0))
        def _():
            z_copy(i, z + 1, z_send).start()

        @pl.when(z > middle + 1)
        def _():
            z_copy(i, z - 1, z_send).start()

        sib_copy(i).start()

    def tile(r):
        return pl.ds((r if r < rb - 1 else rb) * nb, nb)

    solved = pl.ds((rb - 1) * nb, nb)

    def chosen_rows(c, k):
        return apr[c, pl.ds(k * half, half), :, :].reshape(nb, nb)

    def block(c):
        return col if c == 0 else c * 2 * nz + col

    def upper(k):
        return jnp.where(lane >= sub, inv[k], 0.0)

    def lower(k):
        return jnp.where(lane < sub, inv[k], 0.0) + jnp.where(lane == sub, 1.0, 0.0)

    def solve_first():
        w0[...] = weights(upper(0))
        for c in range(cb):
            u[c, pl.ds(0, nb), :] = jnp.where(block(c) > 0, product(lower(0), chosen_rows(c, 0)), 0.0)

    def solve_corner():
        sib_wait(rb - 1)
        corner[...] = product(panel[0, solved, :], upper(0))
        u01 = product(lower(0), panel[1, solved, :])
        cross = product(product(upper(0), u01), upper(1))
        w1[...] = weights(down(-cross, upper(1)))

    def solve_second():
        for c in range(cb):
            left = chosen_rows(c, 1) - product(corner[...], u[c, pl.ds(0, nb), :])
            u[c, pl.ds(nb, nb), :] = jnp.where(block(c) > 1, product(lower(1), left), 0.0)
            wu[:, pl.ds(c * nb, nb)] = weights(u[c])

    def store(r, c):
        return pltpu.make_async_copy(
            a.at[c, pl.ds(r * nb, nb), :], out.at[r, 0, :, c, 0, :], out_sem.at[r * cb + c]
        )

    def update(r):
        sib_wait(r if r < rb - 1 else rb)
        at = pl.ds(r * nb, nb)
        part = r * np_ + me
        c0h, c0l = parts2(panel[0, tile(r), :])
        c1h, c1l = parts2(panel[1, tile(r), :])
        l0 = mul(across(c0h, c0h, c0l), w0[...])
        l1 = mul(across(c0h, c1h, c0h, c1h, c0l, c1l), w1[...])
        if r == 0:
            l0 = jnp.where(me == 0, 0.0, jnp.where(me == 1, corner[...], l0))
            l1 = jnp.where(me <= 1, 0.0, l1)
        high, low = parts2(across(l0, l1))
        change = mul(across(high, high, low), wu[...])
        for c in range(cb):
            total = a[c, at, :]
            if r == 0:
                total = jnp.where(me == 0, chosen_rows(c, 0), jnp.where(me == 1, chosen_rows(c, 1), total))
            total = total - change[:, c * nb : (c + 1) * nb]
            if r == 0:
                for k in range(2):
                    mine = jnp.logical_and(part == k, block(c) > k)
                    total = jnp.where(mine, u[c, pl.ds(k * nb, nb), :], total)
            if c == 0:
                for k, l in enumerate((l0, l1)):
                    total = jnp.where(jnp.logical_and(col == k, part > k), l, total)
            a[c, at, :] = total
            store(r, c).start()

    load(0, 0).wait()
    pl.semaphore_wait(barrier, np_ - 1 + 3)
    old_scatter(0)
    for r in range(1, rb):
        load(r, 0).wait()
    pick(0)
    old_ready(0)
    gather(*old_g, 0)
    rs_start(0)
    for c in range(1, cb):
        for r in range(rb):
            load(r, c).wait()
        old_scatter(c)
    load_inv.wait()

    @pl.when(z == 0)
    def _():
        gather_wait(*old_g, 0)
        old_drain(0)
        old_parts(0)
        for r in range(rb):
            place(0, r)
            panel[core, tile(r), :] = a[0, pl.ds(r * nb, nb), :]
            if r < rb - 1:
                loop(r * PIECE_OF_BLOCK, (r + 1) * PIECE_OF_BLOCK, send)
        rs_finish(0)
        gather(*pr_g, 0)
        for c in range(1, cb):
            pick(c)
            old_ready(c)
        gather_wait(*pr_g, 0)
        for k in range(2):
            @pl.when(core == k)
            def _():
                panel[core, solved, :] = chosen_rows(0, 1 - k)
        loop(early, chunks, send)
        for c in range(1, cb):
            rs_start(c)
            gather(*old_g, c)
            rs_finish(c)
            gather(*pr_g, c)

    @pl.when(z != 0)
    def _():
        for c in range(1, cb):
            pick(c)
            rs_start(c)
            old_ready(c)
            gather(*old_g, c)

    def place_all(c):
        gather_wait(*old_g, c)
        old_drain(c)
        old_parts(c)
        for r in range(rb):
            place(c, r)

    def first_column():
        @pl.when(z != 0)
        def _():
            place_all(0)

    def second_column():
        for c in range(1, cb):
            place_all(c)

    def rows_here():
        @pl.when(z != 0)
        def _():
            gather_wait(*pr_g, 0)

        for c in range(1, cb):
            gather_wait(*pr_g, c)
        solve_first()

    def early_tiles():
        for r in range(rb - 1):
            update(r)

    near = jnp.where(z > middle, nz - z, z)
    turn = jnp.where(near < 5, 14 - 3 * near, 0)
    begin = 33 - 3 * near
    finish = jnp.where(near < middle - 1, chunks, early + PIECE_OF_BLOCK + 1)
    finish = jnp.where(begin + 15 > finish, begin + 15, finish)
    jobs = (
        (begin, first_column), (begin + 3, second_column), (begin + 14, rows_here),
        (finish, solve_corner), (finish + 1, solve_second), (finish + 2, early_tiles),
    )

    def step(i):
        @pl.when(jnp.logical_and(z != 0, i == turn))
        def _():
            for c in range(cb):
                rs_finish(c)
                gather(*pr_g, c)

        @pl.when(jnp.logical_and(z != 0, i < chunks))
        def _():
            relay(i)

        for when, job in jobs:
            pl.when(i == when)(job)

    loop(0, chunks + EXTRA, step)
    update(rb - 1)

    for c in range(cb):
        peers(rs, rs_send, rs_recv, c).wait_send()
        peers(*old_g, c).wait_send()
        peers(*pr_g, c).wait_send()
    whole = panel.at[core]

    def sent(sem):
        pltpu.make_async_remote_copy(whole, whole, sem, z_recv.at[0], device_id=at_col(z, 1 - core)).wait_send()

    sent(sib_send)

    @pl.when(jnp.logical_or(z < middle, z > middle + 1))
    def _():
        sent(z_send)

    @pl.when(z == 0)
    def _():
        sent(z_send2)

    for r in range(rb):
        for c in range(cb):
            store(r, c).wait()


def shards(proc_rows, proc_cols, matrix, pivots, inverse_blocks):
    rb, _, nb, cb, _, _ = matrix.shape
    nz = proc_cols // 2
    rows, slots = rb * nb, 2 * nb
    ch, co = slots // proc_rows, nb // proc_rows
    chunks = (rb + 1) * PIECE_OF_BLOCK
    dma = pltpu.SemaphoreType.DMA
    far = pl.BlockSpec(memory_space=pltpu.HBM)
    pair = dma((cb,))
    return pl.pallas_call(
        functools.partial(kernel, (rb, cb, nb, proc_rows, nz)),
        out_shape=jax.ShapeDtypeStruct(matrix.shape, F32),
        in_specs=[far, far, far],
        out_specs=pl.BlockSpec(memory_space=pl.ANY),
        scratch_shapes=[
            pltpu.VMEM(pivots.shape, jnp.int32),
            pltpu.VMEM(inverse_blocks.shape, F32),
            pltpu.VMEM((cb, rows, nb), F32),
            pltpu.VMEM((3, rows, nb), BF16),
            pltpu.VMEM((cb, slots, nb), F32),
            pltpu.VMEM((cb, proc_rows, ch, nb), F32),
            pltpu.VMEM((cb, proc_rows, 2 * co, nb), F32),
            pltpu.VMEM((cb, proc_rows, ch, nb), F32),
            pltpu.VMEM((2, rows + nb, nb), F32),
            pltpu.VMEM((nb, nb), F32),
            pltpu.VMEM((cb, slots, nb), F32),
            pltpu.VMEM((3 * nb, nb), BF16),
            pltpu.VMEM((6 * nb, nb), BF16),
            pltpu.VMEM((6 * nb, cb * nb), BF16),
            pltpu.VMEM((3, slots, nb), BF16),
            dma((rb * cb + 2,)), dma((rb * cb,)),
            pair, pair, pair, dma((cb, 2)), pair, pair, pair, pair,
            dma, dma, dma((chunks,)), dma, dma((rb + 1,)),
        ],
        compiler_params=pltpu.CompilerParams(
            collective_id=0, has_side_effects=True, vmem_limit_bytes=50 * 2**20
        ),
    )(matrix, pivots, inverse_blocks)


def solution(mesh):
    spec = P(None, "prow", None, None, "pcol", None)
    return jax.shard_map(
        functools.partial(shards, mesh.shape["prow"], mesh.shape["pcol"]),
        mesh=mesh,
        in_specs=(spec, P(), P()),
        out_specs=spec,
        check_vma=False,
    )
```

```python
import functools

import jax
import jax.numpy as jnp
from jax import lax
from jax.experimental import pallas as pl
from jax.experimental.pallas import tpu as pltpu
from jax.sharding import PartitionSpec as P

F32, BF16 = jnp.float32, jnp.bfloat16
PIECE_OF_BLOCK = 8
OLD_AT, ROWS_AT = 4, 18


def mul(left, right):
    return jnp.dot(left, right, preferred_element_type=F32)


def parts2(x):
    high = x.astype(BF16)
    return high, (x - high.astype(F32)).astype(BF16)


def parts3(x):
    high = x.astype(BF16)
    rest = x - high.astype(F32)
    mid = rest.astype(BF16)
    return high, mid, (rest - mid.astype(F32)).astype(BF16)


def across(*x):
    return jnp.concatenate(x, axis=1)


def down(*x):
    return jnp.concatenate(x, axis=0)


def weights(x):
    high, low = parts2(x)
    return down(high, low, high)


def product(left, right):
    high, low = parts2(left)
    return mul(across(high, high, low), weights(right))


def kernel(
    sizes, x, piv_in, inv_in, out,
    piv, inv, a, split, picks, rs, aold, apr, panel, cor, l10, u, w0, w1, wu, old, cold,
    in_sem, out_sem, rs_send, rs_recv, old_send, old_recv, aold_send, aold_recv, apr_send, apr_recv,
    z_send, z_send2, zc_send, zc_send2, z_recv, sib_send, sib_recv, cor_send, cor_recv, sibc_send, sibc_recv,
):
    rb, cb, nb, np_, nz = sizes
    rows, slots = rb * nb, 2 * nb
    ch, co = slots // np_, nb // np_
    half = np_ // 2
    piece = nb // PIECE_OF_BLOCK
    chunks = rb * PIECE_OF_BLOCK
    me = lax.axis_index("prow")
    col = lax.axis_index("pcol")
    z, core = col // 2, col % 2
    middle = nz // 2

    def at_row(r):
        return {"prow": r, "pcol": col}

    def at_col(zz, cc):
        return {"prow": me, "pcol": zz * 2 + cc}

    def loop(low, high, body):
        def step(d, carry):
            body(d)
            return carry

        lax.fori_loop(low, high, step, 0)

    def load(r, c):
        return pltpu.make_async_copy(
            x.at[r, 0, :, c, 0, :], a.at[c, pl.ds(r * nb, nb), :], in_sem.at[r * cb + c]
        )

    load_piv = pltpu.make_async_copy(piv_in, piv, in_sem.at[rb * cb])
    load_inv = pltpu.make_async_copy(inv_in, inv, in_sem.at[rb * cb + 1])
    load_piv.start()
    for c in range(cb):
        for r in range(rb):
            load(r, c).start()
    load_inv.start()

    barrier = pltpu.get_barrier_semaphore()
    loop(1, np_, lambda d: pl.semaphore_signal(barrier, inc=1, device_id=at_row((me + d) % np_)))
    for zz, cc in (((z + 1) % nz, core), ((z + nz - 1) % nz, core), (z, 1 - core)):
        pl.semaphore_signal(barrier, inc=1, device_id=at_col(zz, cc))

    load_piv.wait()
    lane = lax.broadcasted_iota(jnp.int32, (nb, nb), 1)
    sub = lax.broadcasted_iota(jnp.int32, (nb, nb), 0)
    p0r, p1r = piv[0:1, :], piv[1:2, :]
    p0c = jnp.max(jnp.where(lane == sub, p0r, -1), axis=1, keepdims=True)
    p1c = jnp.max(jnp.where(lane == sub, p1r, -1), axis=1, keepdims=True)
    same = p1c == p0r
    back = jnp.max(jnp.where(same, lane, -1), axis=1, keepdims=True)
    src0, src1 = p0c, jnp.where(back >= 0, back, p1c)
    hit = jnp.max(jnp.where(p0r == sub + nb, p1c, -1), axis=0, keepdims=True)
    gone = jnp.max(jnp.where(same, 1, 0), axis=0, keepdims=True)
    dst0 = jnp.where(hit >= 0, hit, jnp.where(gone > 0, -1, p0r))
    up = jnp.max(jnp.where(p0c == lane + nb, 1, 0), axis=0, keepdims=True)
    dst1 = jnp.where(up > 0, -1, p1r)

    def old_copy(c, k, d):
        to = (me + d) % np_
        return pltpu.make_async_remote_copy(
            a.at[c, pl.ds(pl.multiple_of(to * co, co), co), :],
            aold.at[c, to, pl.ds(k * co, co), :],
            old_send.at[c], old_recv.at[c, k], device_id=at_row(to),
        )

    def old_scatter(c):
        for k in range(2):
            @pl.when(me == k)
            def _():
                loop(1, np_, lambda d: old_copy(c, k, d).start())
                aold[c, me, pl.ds(k * co, co), :] = a[c, pl.ds(pl.multiple_of(me * co, co), co), :]

    def old_ready(c):
        for k in range(2):
            @pl.when(me != k)
            def _():
                pltpu.make_async_remote_copy(
                    aold.at[c, me, pl.ds(k * co, co), :], aold.at[c, me, pl.ds(k * co, co), :],
                    old_send.at[c], old_recv.at[c, k], device_id=at_row((me + 1) % np_),
                ).wait_recv()

    def old_drain(c):
        for k in range(2):
            @pl.when(me == k)
            def _():
                sent = a.at[c, pl.ds(0, nb - co), :]
                pltpu.make_async_remote_copy(
                    sent, sent, old_send.at[c], old_recv.at[c, k], device_id=at_row((me + 1) % np_)
                ).wait_send()

    def gather(buf, send, recv, c):
        def start(d):
            pltpu.make_async_remote_copy(
                buf.at[c, me], buf.at[c, me], send.at[c], recv.at[c], device_id=at_row((me + d) % np_)
            ).start()

        loop(1, np_, start)

    def peers(buf, send, recv, c):
        others = buf.at[c, pl.ds(0, np_ - 1)]
        return pltpu.make_async_remote_copy(
            others, others, send.at[c], recv.at[c], device_id=at_row((me + 1) % np_)
        )

    def gather_wait(*which):
        peers(*which).wait_recv()

    old_g, pr_g = (aold, aold_send, aold_recv), (apr, apr_send, apr_recv)

    def pick(c):
        def step(r):
            h, m, l = parts3(a[c, pl.ds(pl.multiple_of(r * nb, nb), nb), :])
            split[0, pl.ds(pl.multiple_of(r * nb, nb), nb), :] = h
            split[1, pl.ds(pl.multiple_of(r * nb, nb), nb), :] = m
            split[2, pl.ds(pl.multiple_of(r * nb, nb), nb), :] = l

        loop(0, rb, step)
        for k, src in ((0, src0), (1, src1)):
            chosen = across(*[(src == (r * np_ + me) * nb + lane).astype(F32).astype(BF16) for r in range(rb)])
            picks[c, pl.ds(k * nb, nb), :] = mul(chosen, split[0]) + mul(chosen, split[1]) + mul(chosen, split[2])

    def rs_start(c):
        rs[c, me] = picks[c, pl.ds(pl.multiple_of(me * ch, ch), ch), :]

        def start(d):
            to = (me + d) % np_
            pltpu.make_async_remote_copy(
                picks.at[c, pl.ds(pl.multiple_of(to * ch, ch), ch), :], rs.at[c, me],
                rs_send.at[c], rs_recv.at[c], device_id=at_row(to),
            ).start()

        loop(1, np_, start)

    def rs_finish(c):
        peers(rs, rs_send, rs_recv, c).wait_recv()
        apr[c, me] = jnp.sum(rs[c], axis=0)

    def old_parts(c):
        for k in range(2):
            at = pl.ds(k * nb, nb)
            old[0, at, :], old[1, at, :], old[2, at, :] = parts3(aold[c, :, pl.ds(k * co, co), :].reshape(nb, nb))

    def moves(r):
        here = (r * np_ + me) * nb + sub
        put0, put1 = (dst0 == here).astype(F32), (dst1 == here).astype(F32)
        moved = jnp.max(jnp.maximum(put0, put1), axis=1, keepdims=True) > 0
        return across(put0.astype(BF16), put1.astype(BF16)), moved

    def place(c, r):
        at = pl.ds(r * nb, nb)
        put, moved = moves(r)
        total = mul(put, old[0]) + mul(put, old[1]) + mul(put, old[2])
        a[c, at, :] = jnp.where(moved, total, a[c, at, :])

    def piece_at(i, which):
        return panel.at[which, pl.ds(pl.multiple_of(i * piece, piece), piece), :]

    def corner_at(j):
        return cor.at[core, me, pl.ds(j * ch, ch), :]

    def z_copy(at, k, zz, sem):
        return pltpu.make_async_remote_copy(at, at, sem, z_recv.at[k], device_id=at_col(zz, core))

    def z_both(at, k, plus, minus):
        z_copy(at, k, 1, plus).start()
        z_copy(at, k, nz - 1, minus).start()

    def z_on(at, k, sem):
        z_copy(at, k, z, sem).wait_recv()

        @pl.when(jnp.logical_and(z < middle, z > 0))
        def _():
            z_copy(at, k, z + 1, sem).start()

        @pl.when(z > middle + 1)
        def _():
            z_copy(at, k, z - 1, sem).start()

    def sib_copy(i):
        at = piece_at(i, core)
        return pltpu.make_async_remote_copy(
            at, at, sib_send, sib_recv.at[i // PIECE_OF_BLOCK], device_id=at_col(z, 1 - core)
        )

    def sib_wait(t):
        at = panel.at[1 - core, pl.ds(t * nb, nb), :]
        pltpu.make_async_remote_copy(at, at, sib_send, sib_recv.at[t], device_id=at_col(z, 1 - core)).wait_recv()

    def cor_copy(which):
        at = cor.at[which]
        return pltpu.make_async_remote_copy(at, at, sibc_send, sibc_recv, device_id=at_col(z, 1 - core))

    cor_g = cor, cor_send, cor_recv, core

    def send(i):
        z_both(piece_at(i, core), i, z_send, z_send2)
        sib_copy(i).start()

    def relay(i):
        z_on(piece_at(i, core), i, z_send)
        sib_copy(i).start()

    def chosen_rows(c, k):
        return apr[c, pl.ds(k * half, half), :, :].reshape(nb, nb)

    def block(c):
        return col if c == 0 else c * 2 * nz + col

    def upper(k):
        return jnp.where(lane >= sub, inv[k], 0.0)

    def lower(k):
        return jnp.where(lane < sub, inv[k], 0.0) + jnp.where(lane == sub, 1.0, 0.0)

    def solve_first():
        w0[...] = weights(upper(0))
        for c in range(cb):
            u[c, pl.ds(0, nb), :] = jnp.where(block(c) > 0, product(lower(0), chosen_rows(c, 0)), 0.0)

    def solve_corner():
        first = cor[0, pl.ds(half, half), pl.ds(ch, ch), :].reshape(nb, nb)
        second = cor[1, pl.ds(0, half), pl.ds(ch, ch), :].reshape(nb, nb)
        l10[...] = product(first, upper(0))
        u01 = product(lower(0), second)
        cross = product(product(upper(0), u01), upper(1))
        w1[...] = weights(down(-cross, upper(1)))
        for b in range(2):
            for k in range(2):
                high, low = parts2(cor[b, :, pl.ds(k * co, co), :].reshape(nb, nb))
                cold[0, pl.ds(k * nb, nb), pl.ds(b * nb, nb)] = high
                cold[1, pl.ds(k * nb, nb), pl.ds(b * nb, nb)] = low

    def solve_second():
        for c in range(cb):
            left = chosen_rows(c, 1) - product(l10[...], u[c, pl.ds(0, nb), :])
            u[c, pl.ds(nb, nb), :] = jnp.where(block(c) > 1, product(lower(1), left), 0.0)
            wu[:, pl.ds(c * nb, nb)] = weights(u[c])

    def store(r, c):
        return pltpu.make_async_copy(
            a.at[c, pl.ds(r * nb, nb), :], out.at[r, 0, :, c, 0, :], out_sem.at[r * cb + c]
        )

    def update(r):
        sib_wait(r)
        at = pl.ds(r * nb, nb)
        part = r * np_ + me
        put, moved = moves(r)
        both = jnp.where(moved, mul(put, cold[0]) + mul(put, cold[1]), across(panel[0, at, :], panel[1, at, :]))
        high, low = parts2(both)
        l0 = mul(across(high[:, :nb], high[:, :nb], low[:, :nb]), w0[...])
        l1 = mul(across(high, high, low), w1[...])
        if r == 0:
            l0 = jnp.where(me == 0, 0.0, jnp.where(me == 1, l10[...], l0))
            l1 = jnp.where(me <= 1, 0.0, l1)
        high, low = parts2(across(l0, l1))
        change = mul(across(high, high, low), wu[...])
        for c in range(cb):
            total = a[c, at, :]
            if r == 0:
                total = jnp.where(me == 0, chosen_rows(c, 0), jnp.where(me == 1, chosen_rows(c, 1), total))
            total = total - change[:, c * nb : (c + 1) * nb]
            if r == 0:
                for k in range(2):
                    mine = jnp.logical_and(part == k, block(c) > k)
                    total = jnp.where(mine, u[c, pl.ds(k * nb, nb), :], total)
            if c == 0:
                for k, l in enumerate((l0, l1)):
                    total = jnp.where(jnp.logical_and(col == k, part > k), l, total)
            a[c, at, :] = total
            store(r, c).start()

    load(0, 0).wait()
    pl.semaphore_wait(barrier, np_ - 1 + 3)
    old_scatter(0)
    for r in range(1, rb):
        load(r, 0).wait()

    @pl.when(z == 0)
    def _():
        panel[core] = a[0]
        loop(0, OLD_AT, send)

    pick(0)
    rs_start(0)
    old_ready(0)

    @pl.when(z == 0)
    def _():
        cor[core, me, pl.ds(0, ch), :] = aold[0, me]
        z_both(corner_at(0), chunks, zc_send, zc_send2)
        loop(OLD_AT, ROWS_AT, send)

    gather(*old_g, 0)
    for c in range(1, cb):
        for r in range(rb):
            load(r, c).wait()
        old_scatter(c)
        pick(c)
        rs_start(c)
        old_ready(c)
        gather(*old_g, c)
    load_inv.wait()

    def chosen_ready():
        for c in range(cb):
            rs_finish(c)
            gather(*pr_g, c)

    @pl.when(z == 0)
    def _():
        rs_finish(0)
        cor[core, me, pl.ds(ch, ch), :] = apr[0, me]
        z_both(corner_at(1), chunks + 1, zc_send, zc_send2)
        loop(ROWS_AT, chunks, send)
        gather(*cor_g)
        gather(*pr_g, 0)
        for c in range(1, cb):
            rs_finish(c)
            gather(*pr_g, c)

    @pl.when(z != 0)
    def _():
        near = jnp.where(z > middle, nz - z, z)
        turn = 28 - 3 * near

        def step(i):
            @pl.when(i == turn)
            def _():
                chosen_ready()

            @pl.when(i == OLD_AT)
            def _():
                z_on(corner_at(0), chunks, zc_send)

            @pl.when(i == ROWS_AT)
            def _():
                z_on(corner_at(1), chunks + 1, zc_send)
                gather(*cor_g)

            relay(i)

        loop(0, chunks, step)

    for c in range(cb):
        gather_wait(*old_g, c)
        old_drain(c)
        old_parts(c)
        for r in range(rb):
            place(c, r)
    gather_wait(*cor_g)
    cor_copy(core).start()
    for c in range(cb):
        gather_wait(*pr_g, c)
    solve_first()
    cor_copy(1 - core).wait_recv()
    solve_corner()
    solve_second()
    for r in range(rb):
        update(r)

    for c in range(cb):
        peers(rs, rs_send, rs_recv, c).wait_send()
        peers(*old_g, c).wait_send()
        peers(*pr_g, c).wait_send()
    peers(*cor_g).wait_send()
    cor_copy(core).wait_send()

    def sent(at, sem):
        z_copy(at, 0, z, sem).wait_send()

    sent(panel.at[core], sib_send)

    @pl.when(jnp.logical_or(z < middle, z > middle + 1))
    def _():
        sent(panel.at[core], z_send)
        sent(cor.at[core, me], zc_send)

    @pl.when(z == 0)
    def _():
        sent(panel.at[core], z_send2)
        sent(cor.at[core, me], zc_send2)

    for r in range(rb):
        for c in range(cb):
            store(r, c).wait()


def shards(proc_rows, proc_cols, matrix, pivots, inverse_blocks):
    rb, _, nb, cb, _, _ = matrix.shape
    nz = proc_cols // 2
    rows, slots = rb * nb, 2 * nb
    ch, co = slots // proc_rows, nb // proc_rows
    chunks = rb * PIECE_OF_BLOCK
    dma = pltpu.SemaphoreType.DMA
    far = pl.BlockSpec(memory_space=pltpu.HBM)
    pair = dma((cb,))
    return pl.pallas_call(
        functools.partial(kernel, (rb, cb, nb, proc_rows, nz)),
        out_shape=jax.ShapeDtypeStruct(matrix.shape, F32),
        in_specs=[far, far, far],
        out_specs=pl.BlockSpec(memory_space=pl.ANY),
        scratch_shapes=[
            pltpu.VMEM(pivots.shape, jnp.int32),
            pltpu.VMEM(inverse_blocks.shape, F32),
            pltpu.VMEM((cb, rows, nb), F32),
            pltpu.VMEM((3, rows, nb), BF16),
            pltpu.VMEM((cb, slots, nb), F32),
            pltpu.VMEM((cb, proc_rows, ch, nb), F32),
            pltpu.VMEM((cb, proc_rows, 2 * co, nb), F32),
            pltpu.VMEM((cb, proc_rows, ch, nb), F32),
            pltpu.VMEM((2, rows, nb), F32),
            pltpu.VMEM((2, proc_rows, 2 * ch, nb), F32),
            pltpu.VMEM((nb, nb), F32),
            pltpu.VMEM((cb, slots, nb), F32),
            pltpu.VMEM((3 * nb, nb), BF16),
            pltpu.VMEM((6 * nb, nb), BF16),
            pltpu.VMEM((6 * nb, cb * nb), BF16),
            pltpu.VMEM((3, slots, nb), BF16),
            pltpu.VMEM((2, slots, 2 * nb), BF16),
            dma((rb * cb + 2,)), dma((rb * cb,)),
            pair, pair, pair, dma((cb, 2)), pair, pair, pair, pair,
            dma, dma, dma, dma, dma((chunks + 2,)), dma, dma((rb,)), dma((2,)), dma((2,)), dma, dma,
        ],
        compiler_params=pltpu.CompilerParams(
            collective_id=0, has_side_effects=True, vmem_limit_bytes=50 * 2**20
        ),
    )(matrix, pivots, inverse_blocks)


def solution(mesh):
    spec = P(None, "prow", None, None, "pcol", None)
    return jax.shard_map(
        functools.partial(shards, mesh.shape["prow"], mesh.shape["pcol"]),
        mesh=mesh,
        in_specs=(spec, P(), P()),
        out_specs=spec,
        check_vma=False,
    )
```

```python
import functools

import jax
import jax.numpy as jnp
from jax import lax
from jax.experimental import pallas as pl
from jax.experimental.pallas import tpu as pltpu
from jax.sharding import PartitionSpec as P

F32, BF16 = jnp.float32, jnp.bfloat16
PIECE_OF_BLOCK = 8
OLD_AT, ROWS_AT, PLACE_AT = 4, 18, 24


def mul(left, right):
    return jnp.dot(left, right, preferred_element_type=F32)


def parts2(x):
    high = x.astype(BF16)
    return high, (x - high.astype(F32)).astype(BF16)


def parts3(x):
    high = x.astype(BF16)
    rest = x - high.astype(F32)
    mid = rest.astype(BF16)
    return high, mid, (rest - mid.astype(F32)).astype(BF16)


def across(*x):
    return jnp.concatenate(x, axis=1)


def down(*x):
    return jnp.concatenate(x, axis=0)


def weights(x):
    high, low = parts2(x)
    return down(high, low, high)


def product(left, right):
    high, low = parts2(left)
    return mul(across(high, high, low), weights(right))


def kernel(
    sizes, x, piv_in, inv_in, out,
    piv, inv, a, split, picks, rs, aold, apr, panel, cor, l10, u, w0, w1, wu, old, cold,
    in_sem, out_sem, rs_send, rs_recv, old_send, old_recv, aold_send, aold_recv, apr_send, apr_recv,
    z_send, z_send2, zc_send, zc_send2, z_recv, sib_send, sib_recv, cor_send, cor_recv, sibc_send, sibc_recv,
):
    rb, cb, nb, np_, nz = sizes
    rows, slots = rb * nb, 2 * nb
    ch, co = slots // np_, nb // np_
    half = np_ // 2
    piece = nb // PIECE_OF_BLOCK
    chunks = rb * PIECE_OF_BLOCK
    me = lax.axis_index("prow")
    col = lax.axis_index("pcol")
    z, core = col // 2, col % 2
    middle = nz // 2

    def at_row(r):
        return {"prow": r, "pcol": col}

    def at_col(zz, cc):
        return {"prow": me, "pcol": zz * 2 + cc}

    def loop(low, high, body):
        def step(d, carry):
            body(d)
            return carry

        lax.fori_loop(low, high, step, 0)

    def load(r, c):
        return pltpu.make_async_copy(
            x.at[r, 0, :, c, 0, :], a.at[c, pl.ds(r * nb, nb), :], in_sem.at[r * cb + c]
        )

    load_piv = pltpu.make_async_copy(piv_in, piv, in_sem.at[rb * cb])
    load_inv = pltpu.make_async_copy(inv_in, inv, in_sem.at[rb * cb + 1])
    load_piv.start()
    for c in range(cb):
        for r in range(rb):
            load(r, c).start()
    load_inv.start()

    barrier = pltpu.get_barrier_semaphore()
    loop(1, np_, lambda d: pl.semaphore_signal(barrier, inc=1, device_id=at_row((me + d) % np_)))
    pl.semaphore_signal(barrier, inc=1, device_id=at_col(z, 1 - core))

    @pl.when(z == 0)
    def _():
        loop(1, nz, lambda zz: pl.semaphore_signal(barrier, inc=1, device_id=at_col(zz, core)))

    @pl.when(z != 0)
    def _():
        pl.semaphore_signal(barrier, inc=1, device_id=at_col(0, core))

    @pl.when(z > 1)
    def _():
        pl.semaphore_signal(barrier, inc=1, device_id=at_col(z - 1, core))

    @pl.when(jnp.logical_and(z > 0, z < nz - 1))
    def _():
        pl.semaphore_signal(barrier, inc=1, device_id=at_col(z + 1, core))

    load_piv.wait()
    lane = lax.broadcasted_iota(jnp.int32, (nb, nb), 1)
    sub = lax.broadcasted_iota(jnp.int32, (nb, nb), 0)
    p0r, p1r = piv[0:1, :], piv[1:2, :]
    p0c = jnp.max(jnp.where(lane == sub, p0r, -1), axis=1, keepdims=True)
    p1c = jnp.max(jnp.where(lane == sub, p1r, -1), axis=1, keepdims=True)
    same = p1c == p0r
    back = jnp.max(jnp.where(same, lane, -1), axis=1, keepdims=True)
    src0, src1 = p0c, jnp.where(back >= 0, back, p1c)
    hit = jnp.max(jnp.where(p0r == sub + nb, p1c, -1), axis=0, keepdims=True)
    gone = jnp.max(jnp.where(same, 1, 0), axis=0, keepdims=True)
    dst0 = jnp.where(hit >= 0, hit, jnp.where(gone > 0, -1, p0r))
    up = jnp.max(jnp.where(p0c == lane + nb, 1, 0), axis=0, keepdims=True)
    dst1 = jnp.where(up > 0, -1, p1r)

    def old_copy(c, k, d):
        to = (me + d) % np_
        return pltpu.make_async_remote_copy(
            a.at[c, pl.ds(pl.multiple_of(to * co, co), co), :],
            aold.at[c, to, pl.ds(k * co, co), :],
            old_send.at[c], old_recv.at[c, k], device_id=at_row(to),
        )

    def old_scatter(c):
        for k in range(2):
            @pl.when(me == k)
            def _():
                loop(1, np_, lambda d: old_copy(c, k, d).start())
                aold[c, me, pl.ds(k * co, co), :] = a[c, pl.ds(pl.multiple_of(me * co, co), co), :]

    def old_ready(c):
        for k in range(2):
            @pl.when(me != k)
            def _():
                pltpu.make_async_remote_copy(
                    aold.at[c, me, pl.ds(k * co, co), :], aold.at[c, me, pl.ds(k * co, co), :],
                    old_send.at[c], old_recv.at[c, k], device_id=at_row((me + 1) % np_),
                ).wait_recv()

    def old_drain(c):
        for k in range(2):
            @pl.when(me == k)
            def _():
                sent = a.at[c, pl.ds(0, nb - co), :]
                pltpu.make_async_remote_copy(
                    sent, sent, old_send.at[c], old_recv.at[c, k], device_id=at_row((me + 1) % np_)
                ).wait_send()

    def gather(buf, send, recv, c):
        def start(d):
            pltpu.make_async_remote_copy(
                buf.at[c, me], buf.at[c, me], send.at[c], recv.at[c], device_id=at_row((me + d) % np_)
            ).start()

        loop(1, np_, start)

    def peers(buf, send, recv, c):
        others = buf.at[c, pl.ds(0, np_ - 1)]
        return pltpu.make_async_remote_copy(
            others, others, send.at[c], recv.at[c], device_id=at_row((me + 1) % np_)
        )

    def gather_wait(*which):
        peers(*which).wait_recv()

    old_g, pr_g = (aold, aold_send, aold_recv), (apr, apr_send, apr_recv)

    def pick(c):
        def step(r):
            h, m, l = parts3(a[c, pl.ds(pl.multiple_of(r * nb, nb), nb), :])
            split[0, pl.ds(pl.multiple_of(r * nb, nb), nb), :] = h
            split[1, pl.ds(pl.multiple_of(r * nb, nb), nb), :] = m
            split[2, pl.ds(pl.multiple_of(r * nb, nb), nb), :] = l

        loop(0, rb, step)
        for k, src in ((0, src0), (1, src1)):
            chosen = across(*[(src == (r * np_ + me) * nb + lane).astype(F32).astype(BF16) for r in range(rb)])
            picks[c, pl.ds(k * nb, nb), :] = mul(chosen, split[0]) + mul(chosen, split[1]) + mul(chosen, split[2])

    def rs_start(c):
        rs[c, me] = picks[c, pl.ds(pl.multiple_of(me * ch, ch), ch), :]

        def start(d):
            to = (me + d) % np_
            pltpu.make_async_remote_copy(
                picks.at[c, pl.ds(pl.multiple_of(to * ch, ch), ch), :], rs.at[c, me],
                rs_send.at[c], rs_recv.at[c], device_id=at_row(to),
            ).start()

        loop(1, np_, start)

    def rs_finish(c):
        peers(rs, rs_send, rs_recv, c).wait_recv()
        apr[c, me] = jnp.sum(rs[c], axis=0)

    def old_parts(c):
        for k in range(2):
            at = pl.ds(k * nb, nb)
            old[0, at, :], old[1, at, :], old[2, at, :] = parts3(aold[c, :, pl.ds(k * co, co), :].reshape(nb, nb))

    def moves(r):
        here = (r * np_ + me) * nb + sub
        put0, put1 = (dst0 == here).astype(F32), (dst1 == here).astype(F32)
        moved = jnp.max(jnp.maximum(put0, put1), axis=1, keepdims=True) > 0
        return across(put0.astype(BF16), put1.astype(BF16)), moved

    def place(c, r):
        at = pl.ds(r * nb, nb)
        put, moved = moves(r)
        total = mul(put, old[0]) + mul(put, old[1]) + mul(put, old[2])
        a[c, at, :] = jnp.where(moved, total, a[c, at, :])

    def piece_at(i, which):
        return panel.at[which, pl.ds(pl.multiple_of(i * piece, piece), piece), :]

    def corner_at(j):
        return cor.at[core, me, pl.ds(j * ch, ch), :]

    def z_copy(at, k, zz, sem):
        return pltpu.make_async_remote_copy(at, at, sem, z_recv.at[k], device_id=at_col(zz, core))

    def z_both(at, k, plus, minus):
        z_copy(at, k, 1, plus).start()
        z_copy(at, k, nz - 1, minus).start()

    def z_on(at, k, sem):
        z_copy(at, k, z, sem).wait_recv()

        @pl.when(jnp.logical_and(z < middle, z > 0))
        def _():
            z_copy(at, k, z + 1, sem).start()

        @pl.when(z > middle + 1)
        def _():
            z_copy(at, k, z - 1, sem).start()

    def sib_copy(i):
        at = piece_at(i, core)
        return pltpu.make_async_remote_copy(
            at, at, sib_send, sib_recv.at[i // PIECE_OF_BLOCK], device_id=at_col(z, 1 - core)
        )

    def sib_wait(t):
        at = panel.at[1 - core, pl.ds(t * nb, nb), :]
        pltpu.make_async_remote_copy(at, at, sib_send, sib_recv.at[t], device_id=at_col(z, 1 - core)).wait_recv()

    def cor_copy(which):
        at = cor.at[which]
        return pltpu.make_async_remote_copy(at, at, sibc_send, sibc_recv, device_id=at_col(z, 1 - core))

    cor_g = cor, cor_send, cor_recv, core

    def send(i):
        z_both(piece_at(i, core), i, z_send, z_send2)
        sib_copy(i).start()

    def relay(i):
        z_on(piece_at(i, core), i, z_send)
        sib_copy(i).start()

    def chosen_rows(c, k):
        return apr[c, pl.ds(k * half, half), :, :].reshape(nb, nb)

    def block(c):
        return col if c == 0 else c * 2 * nz + col

    def upper(k):
        return jnp.where(lane >= sub, inv[k], 0.0)

    def lower(k):
        return jnp.where(lane < sub, inv[k], 0.0) + jnp.where(lane == sub, 1.0, 0.0)

    def solve_first():
        w0[...] = weights(upper(0))
        for c in range(cb):
            u[c, pl.ds(0, nb), :] = jnp.where(block(c) > 0, product(lower(0), chosen_rows(c, 0)), 0.0)

    def solve_corner():
        first = cor[0, pl.ds(half, half), pl.ds(ch, ch), :].reshape(nb, nb)
        second = cor[1, pl.ds(0, half), pl.ds(ch, ch), :].reshape(nb, nb)
        l10[...] = product(first, upper(0))
        u01 = product(lower(0), second)
        cross = product(product(upper(0), u01), upper(1))
        w1[...] = weights(down(-cross, upper(1)))
        for b in range(2):
            for k in range(2):
                high, low = parts2(cor[b, :, pl.ds(k * co, co), :].reshape(nb, nb))
                cold[0, pl.ds(k * nb, nb), pl.ds(b * nb, nb)] = high
                cold[1, pl.ds(k * nb, nb), pl.ds(b * nb, nb)] = low

    def solve_second():
        for c in range(cb):
            left = chosen_rows(c, 1) - product(l10[...], u[c, pl.ds(0, nb), :])
            u[c, pl.ds(nb, nb), :] = jnp.where(block(c) > 1, product(lower(1), left), 0.0)
            wu[:, pl.ds(c * nb, nb)] = weights(u[c])

    def store(r, c):
        return pltpu.make_async_copy(
            a.at[c, pl.ds(r * nb, nb), :], out.at[r, 0, :, c, 0, :], out_sem.at[r * cb + c]
        )

    def update(r):
        sib_wait(r)
        at = pl.ds(r * nb, nb)
        part = r * np_ + me
        put, moved = moves(r)
        both = jnp.where(moved, mul(put, cold[0]) + mul(put, cold[1]), across(panel[0, at, :], panel[1, at, :]))
        high, low = parts2(both)
        l0 = mul(across(high[:, :nb], high[:, :nb], low[:, :nb]), w0[...])
        l1 = mul(across(high, high, low), w1[...])
        if r == 0:
            l0 = jnp.where(me == 0, 0.0, jnp.where(me == 1, l10[...], l0))
            l1 = jnp.where(me <= 1, 0.0, l1)
        high, low = parts2(across(l0, l1))
        change = mul(across(high, high, low), wu[...])
        for c in range(cb):
            total = a[c, at, :]
            if r == 0:
                total = jnp.where(me == 0, chosen_rows(c, 0), jnp.where(me == 1, chosen_rows(c, 1), total))
            total = total - change[:, c * nb : (c + 1) * nb]
            if r == 0:
                for k in range(2):
                    mine = jnp.logical_and(part == k, block(c) > k)
                    total = jnp.where(mine, u[c, pl.ds(k * nb, nb), :], total)
            if c == 0:
                for k, l in enumerate((l0, l1)):
                    total = jnp.where(jnp.logical_and(col == k, part > k), l, total)
            a[c, at, :] = total
            store(r, c).start()

    load(0, 0).wait()
    @pl.when(z == 0)
    def _():
        pl.semaphore_wait(barrier, np_ + nz - 1)

    @pl.when(jnp.logical_or(z == 1, z == nz - 1))
    def _():
        pl.semaphore_wait(barrier, np_ + 2)

    @pl.when(jnp.logical_and(z > 1, z < nz - 1))
    def _():
        pl.semaphore_wait(barrier, np_ + 3)

    old_scatter(0)
    for r in range(1, rb):
        load(r, 0).wait()

    @pl.when(z == 0)
    def _():
        panel[core] = a[0]
        loop(0, OLD_AT, send)

    pick(0)
    rs_start(0)
    old_ready(0)

    @pl.when(z == 0)
    def _():
        cor[core, me, pl.ds(0, ch), :] = aold[0, me]
        z_both(corner_at(0), chunks, zc_send, zc_send2.at[0])
        loop(OLD_AT, ROWS_AT, send)

    gather(*old_g, 0)
    for c in range(1, cb):
        for r in range(rb):
            load(r, c).wait()
        old_scatter(c)
        pick(c)
        rs_start(c)
        old_ready(c)
        gather(*old_g, c)
    load_inv.wait()

    def corner_to(zz):
        return z_copy(corner_at(1), chunks + 1, zz, zc_send2.at[zz])

    def place_all():
        for c in range(cb):
            gather_wait(*old_g, c)
            old_drain(c)
            old_parts(c)
            for r in range(rb):
                place(c, r)

    def first_ready():
        rs_finish(0)
        gather(*pr_g, 0)

    def others_ready():
        for c in range(1, cb):
            rs_finish(c)
            gather(*pr_g, c)

    @pl.when(z == 0)
    def _():
        rs_finish(0)
        cor[core, me, pl.ds(ch, ch), :] = apr[0, me]
        loop(1, nz, lambda zz: corner_to(zz).start())
        loop(ROWS_AT, chunks, send)
        gather(*cor_g)
        gather(*pr_g, 0)
        others_ready()
        place_all()

    @pl.when(z != 0)
    def _():
        near = jnp.where(z > middle, nz - z, z)
        turn = jnp.where(near < 2, PLACE_AT - 1, 28 - 3 * near)

        def step(i):
            @pl.when(i == OLD_AT)
            def _():
                z_on(corner_at(0), chunks, zc_send)

            @pl.when(i == turn)
            def _():
                first_ready()
                corner_to(z).wait_recv()
                gather(*cor_g)
                others_ready()

            relay(i)

        loop(0, PLACE_AT, step)
        place_all()
        loop(PLACE_AT, chunks, step)

    gather_wait(*cor_g)
    cor_copy(core).start()
    for c in range(cb):
        gather_wait(*pr_g, c)
    solve_first()
    cor_copy(1 - core).wait_recv()
    solve_corner()
    solve_second()
    for r in range(rb):
        update(r)

    for c in range(cb):
        peers(rs, rs_send, rs_recv, c).wait_send()
        peers(*old_g, c).wait_send()
        peers(*pr_g, c).wait_send()
    peers(*cor_g).wait_send()
    cor_copy(core).wait_send()

    def sent(at, sem):
        z_copy(at, 0, z, sem).wait_send()

    sent(panel.at[core], sib_send)

    @pl.when(jnp.logical_or(z < middle, z > middle + 1))
    def _():
        sent(panel.at[core], z_send)
        sent(corner_at(0), zc_send)

    @pl.when(z == 0)
    def _():
        sent(panel.at[core], z_send2)
        sent(corner_at(0), zc_send2.at[0])
        loop(1, nz, lambda zz: corner_to(zz).wait_send())

    for r in range(rb):
        for c in range(cb):
            store(r, c).wait()


def shards(proc_rows, proc_cols, matrix, pivots, inverse_blocks):
    rb, _, nb, cb, _, _ = matrix.shape
    nz = proc_cols // 2
    rows, slots = rb * nb, 2 * nb
    ch, co = slots // proc_rows, nb // proc_rows
    chunks = rb * PIECE_OF_BLOCK
    dma = pltpu.SemaphoreType.DMA
    far = pl.BlockSpec(memory_space=pltpu.HBM)
    pair = dma((cb,))
    return pl.pallas_call(
        functools.partial(kernel, (rb, cb, nb, proc_rows, nz)),
        out_shape=jax.ShapeDtypeStruct(matrix.shape, F32),
        in_specs=[far, far, far],
        out_specs=pl.BlockSpec(memory_space=pl.ANY),
        scratch_shapes=[
            pltpu.VMEM(pivots.shape, jnp.int32),
            pltpu.VMEM(inverse_blocks.shape, F32),
            pltpu.VMEM((cb, rows, nb), F32),
            pltpu.VMEM((3, rows, nb), BF16),
            pltpu.VMEM((cb, slots, nb), F32),
            pltpu.VMEM((cb, proc_rows, ch, nb), F32),
            pltpu.VMEM((cb, proc_rows, 2 * co, nb), F32),
            pltpu.VMEM((cb, proc_rows, ch, nb), F32),
            pltpu.VMEM((2, rows, nb), F32),
            pltpu.VMEM((2, proc_rows, 2 * ch, nb), F32),
            pltpu.VMEM((nb, nb), F32),
            pltpu.VMEM((cb, slots, nb), F32),
            pltpu.VMEM((3 * nb, nb), BF16),
            pltpu.VMEM((6 * nb, nb), BF16),
            pltpu.VMEM((6 * nb, cb * nb), BF16),
            pltpu.VMEM((3, slots, nb), BF16),
            pltpu.VMEM((2, slots, 2 * nb), BF16),
            dma((rb * cb + 2,)), dma((rb * cb,)),
            pair, pair, pair, dma((cb, 2)), pair, pair, pair, pair,
            dma, dma, dma, dma((nz,)), dma((chunks + 2,)), dma, dma((rb,)), dma((2,)), dma((2,)), dma, dma,
        ],
        compiler_params=pltpu.CompilerParams(
            collective_id=0, has_side_effects=True, vmem_limit_bytes=50 * 2**20
        ),
    )(matrix, pivots, inverse_blocks)


def solution(mesh):
    spec = P(None, "prow", None, None, "pcol", None)
    return jax.shard_map(
        functools.partial(shards, mesh.shape["prow"], mesh.shape["pcol"]),
        mesh=mesh,
        in_specs=(spec, P(), P()),
        out_specs=spec,
        check_vma=False,
    )
```

```python
import functools

import jax
import jax.numpy as jnp
from jax import lax
from jax.experimental import pallas as pl
from jax.experimental.pallas import tpu as pltpu
from jax.sharding import PartitionSpec as P

F32, BF16 = jnp.float32, jnp.bfloat16
PIECE_OF_BLOCK = 8
EXTRA = 11


def mul(left, right):
    return jnp.dot(left, right, preferred_element_type=F32)


def parts2(x):
    high = x.astype(BF16)
    return high, (x - high.astype(F32)).astype(BF16)


def parts3(x):
    high = x.astype(BF16)
    rest = x - high.astype(F32)
    mid = rest.astype(BF16)
    return high, mid, (rest - mid.astype(F32)).astype(BF16)


def across(*x):
    return jnp.concatenate(x, axis=1)


def down(*x):
    return jnp.concatenate(x, axis=0)


def weights(x):
    high, low = parts2(x)
    return down(high, low, high)


def product(left, right):
    high, low = parts2(left)
    return mul(across(high, high, low), weights(right))


def kernel(
    sizes, x, piv_in, inv_in, out,
    piv, inv, a, split, picks, rs, aold, apr, panel, corner, u, w0, w1, wu, old,
    in_sem, out_sem, rs_send, rs_recv, old_send, old_recv, aold_send, aold_recv, apr_send, apr_recv,
    z_send, z_send2, z_recv, sib_send, sib_recv,
):
    rb, cb, nb, np_, nz = sizes
    rows, slots = rb * nb, 2 * nb
    ch, co = slots // np_, nb // np_
    half = np_ // 2
    piece = nb // PIECE_OF_BLOCK
    chunks = (rb + 1) * PIECE_OF_BLOCK
    early = (rb - 1) * PIECE_OF_BLOCK
    me = lax.axis_index("prow")
    col = lax.axis_index("pcol")
    z, core = col // 2, col % 2
    middle = nz // 2

    def at_row(r):
        return {"prow": r, "pcol": col}

    def at_col(zz, cc):
        return {"prow": me, "pcol": zz * 2 + cc}

    def loop(low, high, body):
        def step(d, carry):
            body(d)
            return carry

        lax.fori_loop(low, high, step, 0)

    def load(r, c):
        return pltpu.make_async_copy(
            x.at[r, 0, :, c, 0, :], a.at[c, pl.ds(r * nb, nb), :], in_sem.at[r * cb + c]
        )

    load_piv = pltpu.make_async_copy(piv_in, piv, in_sem.at[rb * cb])
    load_inv = pltpu.make_async_copy(inv_in, inv, in_sem.at[rb * cb + 1])
    load_piv.start()
    for c in range(cb):
        for r in range(rb):
            load(r, c).start()
    load_inv.start()

    barrier = pltpu.get_barrier_semaphore()
    loop(1, np_, lambda d: pl.semaphore_signal(barrier, inc=1, device_id=at_row((me + d) % np_)))
    for zz, cc in (((z + 1) % nz, core), ((z + nz - 1) % nz, core), (z, 1 - core)):
        pl.semaphore_signal(barrier, inc=1, device_id=at_col(zz, cc))

    load_piv.wait()
    lane = lax.broadcasted_iota(jnp.int32, (nb, nb), 1)
    sub = lax.broadcasted_iota(jnp.int32, (nb, nb), 0)
    p0r, p1r = piv[0:1, :], piv[1:2, :]
    p0c = jnp.max(jnp.where(lane == sub, p0r, -1), axis=1, keepdims=True)
    p1c = jnp.max(jnp.where(lane == sub, p1r, -1), axis=1, keepdims=True)
    same = p1c == p0r
    back = jnp.max(jnp.where(same, lane, -1), axis=1, keepdims=True)
    src0, src1 = p0c, jnp.where(back >= 0, back, p1c)
    hit = jnp.max(jnp.where(p0r == sub + nb, p1c, -1), axis=0, keepdims=True)
    gone = jnp.max(jnp.where(same, 1, 0), axis=0, keepdims=True)
    dst0 = jnp.where(hit >= 0, hit, jnp.where(gone > 0, -1, p0r))
    up = jnp.max(jnp.where(p0c == lane + nb, 1, 0), axis=0, keepdims=True)
    dst1 = jnp.where(up > 0, -1, p1r)

    def old_copy(c, k, d):
        to = (me + d) % np_
        return pltpu.make_async_remote_copy(
            a.at[c, pl.ds(pl.multiple_of(to * co, co), co), :],
            aold.at[c, to, pl.ds(k * co, co), :],
            old_send.at[c], old_recv.at[c, k], device_id=at_row(to),
        )

    def old_scatter(c):
        for k in range(2):
            @pl.when(me == k)
            def _():
                loop(1, np_, lambda d: old_copy(c, k, d).start())
                aold[c, me, pl.ds(k * co, co), :] = a[c, pl.ds(pl.multiple_of(me * co, co), co), :]

    def old_ready(c):
        for k in range(2):
            @pl.when(me != k)
            def _():
                pltpu.make_async_remote_copy(
                    aold.at[c, me, pl.ds(k * co, co), :], aold.at[c, me, pl.ds(k * co, co), :],
                    old_send.at[c], old_recv.at[c, k], device_id=at_row((me + 1) % np_),
                ).wait_recv()

    def old_drain(c):
        for k in range(2):
            @pl.when(me == k)
            def _():
                sent = a.at[c, pl.ds(0, nb - co), :]
                pltpu.make_async_remote_copy(
                    sent, sent, old_send.at[c], old_recv.at[c, k], device_id=at_row((me + 1) % np_)
                ).wait_send()

    def gather(buf, send, recv, c):
        def start(d):
            pltpu.make_async_remote_copy(
                buf.at[c, me], buf.at[c, me], send.at[c], recv.at[c], device_id=at_row((me + d) % np_)
            ).start()

        loop(1, np_, start)

    def peers(buf, send, recv, c):
        others = buf.at[c, pl.ds(0, np_ - 1)]
        return pltpu.make_async_remote_copy(
            others, others, send.at[c], recv.at[c], device_id=at_row((me + 1) % np_)
        )

    def gather_wait(*which):
        peers(*which).wait_recv()

    old_g, pr_g = (aold, aold_send, aold_recv), (apr, apr_send, apr_recv)

    def pick(c):
        def step(r):
            h, m, l = parts3(a[c, pl.ds(pl.multiple_of(r * nb, nb), nb), :])
            split[0, pl.ds(pl.multiple_of(r * nb, nb), nb), :] = h
            split[1, pl.ds(pl.multiple_of(r * nb, nb), nb), :] = m
            split[2, pl.ds(pl.multiple_of(r * nb, nb), nb), :] = l

        loop(0, rb, step)
        for k, src in ((0, src0), (1, src1)):
            chosen = across(*[(src == (r * np_ + me) * nb + lane).astype(F32).astype(BF16) for r in range(rb)])
            picks[c, pl.ds(k * nb, nb), :] = mul(chosen, split[0]) + mul(chosen, split[1]) + mul(chosen, split[2])

    def rs_start(c):
        rs[c, me] = picks[c, pl.ds(pl.multiple_of(me * ch, ch), ch), :]

        def start(d):
            to = (me + d) % np_
            pltpu.make_async_remote_copy(
                picks.at[c, pl.ds(pl.multiple_of(to * ch, ch), ch), :], rs.at[c, me],
                rs_send.at[c], rs_recv.at[c], device_id=at_row(to),
            ).start()

        loop(1, np_, start)

    def rs_finish(c):
        peers(rs, rs_send, rs_recv, c).wait_recv()
        apr[c, me] = jnp.sum(rs[c], axis=0)

    def old_parts(c):
        for k in range(2):
            at = pl.ds(k * nb, nb)
            old[0, at, :], old[1, at, :], old[2, at, :] = parts3(aold[c, :, pl.ds(k * co, co), :].reshape(nb, nb))

    def place(c, r):
        at = pl.ds(r * nb, nb)
        here = (r * np_ + me) * nb + sub
        put0, put1 = (dst0 == here).astype(F32), (dst1 == here).astype(F32)
        moved = jnp.max(jnp.maximum(put0, put1), axis=1, keepdims=True)
        put = across(put0.astype(BF16), put1.astype(BF16))
        total = mul(put, old[0]) + mul(put, old[1]) + mul(put, old[2])
        a[c, at, :] = jnp.where(moved > 0, total, a[c, at, :])

    def piece_at(i, which):
        return panel.at[which, pl.ds(pl.multiple_of(i * piece, piece), piece), :]

    def z_copy(i, zz, sem):
        at = piece_at(i, core)
        return pltpu.make_async_remote_copy(at, at, sem, z_recv.at[i], device_id=at_col(zz, core))

    def sib_copy(i):
        at = piece_at(i, core)
        return pltpu.make_async_remote_copy(
            at, at, sib_send, sib_recv.at[i // PIECE_OF_BLOCK], device_id=at_col(z, 1 - core)
        )

    def sib_wait(t):
        at = panel.at[1 - core, pl.ds(t * nb, nb), :]
        pltpu.make_async_remote_copy(at, at, sib_send, sib_recv.at[t], device_id=at_col(z, 1 - core)).wait_recv()

    def send(i):
        z_copy(i, 1, z_send).start()
        z_copy(i, nz - 1, z_send2).start()
        sib_copy(i).start()

    def relay(i):
        z_copy(i, z, z_send).wait_recv()

        @pl.when(jnp.logical_and(z < middle, z > 0))
        def _():
            z_copy(i, z + 1, z_send).start()

        @pl.when(z > middle + 1)
        def _():
            z_copy(i, z - 1, z_send).start()

        sib_copy(i).start()

    def tile(r):
        return pl.ds((r if r < rb - 1 else rb) * nb, nb)

    solved = pl.ds((rb - 1) * nb, nb)

    def chosen_rows(c, k):
        return apr[c, pl.ds(k * half, half), :, :].reshape(nb, nb)

    def block(c):
        return col if c == 0 else c * 2 * nz + col

    def upper(k):
        return jnp.where(lane >= sub, inv[k], 0.0)

    def lower(k):
        return jnp.where(lane < sub, inv[k], 0.0) + jnp.where(lane == sub, 1.0, 0.0)

    def solve_first():
        w0[...] = weights(upper(0))
        for c in range(cb):
            u[c, pl.ds(0, nb), :] = jnp.where(block(c) > 0, product(lower(0), chosen_rows(c, 0)), 0.0)

    def solve_corner():
        sib_wait(rb - 1)
        corner[...] = product(panel[0, solved, :], upper(0))
        u01 = product(lower(0), panel[1, solved, :])
        cross = product(product(upper(0), u01), upper(1))
        w1[...] = weights(down(-cross, upper(1)))

    def solve_second():
        for c in range(cb):
            left = chosen_rows(c, 1) - product(corner[...], u[c, pl.ds(0, nb), :])
            u[c, pl.ds(nb, nb), :] = jnp.where(block(c) > 1, product(lower(1), left), 0.0)
            wu[:, pl.ds(c * nb, nb)] = weights(u[c])

    def store(r, c):
        return pltpu.make_async_copy(
            a.at[c, pl.ds(r * nb, nb), :], out.at[r, 0, :, c, 0, :], out_sem.at[r * cb + c]
        )

    def update(r):
        sib_wait(r if r < rb - 1 else rb)
        at = pl.ds(r * nb, nb)
        part = r * np_ + me
        c0h, c0l = parts2(panel[0, tile(r), :])
        c1h, c1l = parts2(panel[1, tile(r), :])
        l0 = mul(across(c0h, c0h, c0l), w0[...])
        l1 = mul(across(c0h, c1h, c0h, c1h, c0l, c1l), w1[...])
        if r == 0:
            l0 = jnp.where(me == 0, 0.0, jnp.where(me == 1, corner[...], l0))
            l1 = jnp.where(me <= 1, 0.0, l1)
        high, low = parts2(across(l0, l1))
        change = mul(across(high, high, low), wu[...])
        for c in range(cb):
            total = a[c, at, :]
            if r == 0:
                total = jnp.where(me == 0, chosen_rows(c, 0), jnp.where(me == 1, chosen_rows(c, 1), total))
            total = total - change[:, c * nb : (c + 1) * nb]
            if r == 0:
                for k in range(2):
                    mine = jnp.logical_and(part == k, block(c) > k)
                    total = jnp.where(mine, u[c, pl.ds(k * nb, nb), :], total)
            if c == 0:
                for k, l in enumerate((l0, l1)):
                    total = jnp.where(jnp.logical_and(col == k, part > k), l, total)
            a[c, at, :] = total
            store(r, c).start()

    load(0, 0).wait()
    pl.semaphore_wait(barrier, np_ - 1 + 3)
    old_scatter(0)
    for r in range(1, rb):
        load(r, 0).wait()
    pick(0)
    old_ready(0)
    gather(*old_g, 0)
    rs_start(0)
    for c in range(1, cb):
        for r in range(rb):
            load(r, c).wait()
        old_scatter(c)
    load_inv.wait()

    @pl.when(z == 0)
    def _():
        gather_wait(*old_g, 0)
        old_drain(0)
        old_parts(0)
        for r in range(rb):
            place(0, r)
            panel[core, tile(r), :] = a[0, pl.ds(r * nb, nb), :]
            if r < rb - 1:
                loop(r * PIECE_OF_BLOCK, (r + 1) * PIECE_OF_BLOCK, send)
        rs_finish(0)
        gather(*pr_g, 0)
        for c in range(1, cb):
            pick(c)
            old_ready(c)
        gather_wait(*pr_g, 0)
        for k in range(2):
            @pl.when(core == k)
            def _():
                panel[core, solved, :] = chosen_rows(0, 1 - k)
        loop(early, chunks, send)
        for c in range(1, cb):
            rs_start(c)
            gather(*old_g, c)
            rs_finish(c)
            gather(*pr_g, c)

    @pl.when(z != 0)
    def _():
        for c in range(1, cb):
            pick(c)
            rs_start(c)
            old_ready(c)
            gather(*old_g, c)

    def old_here(c):
        gather_wait(*old_g, c)
        old_drain(c)
        old_parts(c)

    def unless_first(body, *args):
        @pl.when(z != 0)
        def _():
            body(*args)

    def rows_here():
        @pl.when(z != 0)
        def _():
            gather_wait(*pr_g, 0)

        for c in range(1, cb):
            gather_wait(*pr_g, c)
        solve_first()

    def early_tiles():
        for r in range(rb - 1):
            update(r)

    near = jnp.where(z > middle, nz - z, z)
    turn = jnp.where(near < 5, 14 - 3 * near, 0)
    begin = 33 - 3 * near
    last = jnp.logical_or(z == middle, z == middle + 1)
    finish = jnp.where(last, early + PIECE_OF_BLOCK + 1, chunks)
    finish = jnp.where(begin + 15 > finish, begin + 15, finish)
    slices = [functools.partial(unless_first, old_here, 0)]
    slices += [functools.partial(unless_first, place, 0, r) for r in range(rb)]
    for c in range(1, cb):
        slices += [functools.partial(old_here, c)] + [functools.partial(place, c, r) for r in range(rb)]
    jobs = [(begin + j, body) for j, body in enumerate(slices)]
    jobs += [(begin + 14, rows_here), (finish, solve_corner), (finish + 1, solve_second), (finish + 2, early_tiles)]

    def step(i):
        @pl.when(jnp.logical_and(z != 0, i == turn))
        def _():
            for c in range(cb):
                rs_finish(c)
                gather(*pr_g, c)

        @pl.when(jnp.logical_and(z != 0, i < chunks))
        def _():
            relay(i)

        for when, job in jobs:
            pl.when(i == when)(job)

    loop(0, chunks + EXTRA, step)
    update(rb - 1)

    for c in range(cb):
        peers(rs, rs_send, rs_recv, c).wait_send()
        peers(*old_g, c).wait_send()
        peers(*pr_g, c).wait_send()
    whole = panel.at[core]

    def sent(sem):
        pltpu.make_async_remote_copy(whole, whole, sem, z_recv.at[0], device_id=at_col(z, 1 - core)).wait_send()

    sent(sib_send)

    @pl.when(jnp.logical_or(z < middle, z > middle + 1))
    def _():
        sent(z_send)

    @pl.when(z == 0)
    def _():
        sent(z_send2)

    for r in range(rb):
        for c in range(cb):
            store(r, c).wait()


def shards(proc_rows, proc_cols, matrix, pivots, inverse_blocks):
    rb, _, nb, cb, _, _ = matrix.shape
    nz = proc_cols // 2
    rows, slots = rb * nb, 2 * nb
    ch, co = slots // proc_rows, nb // proc_rows
    chunks = (rb + 1) * PIECE_OF_BLOCK
    dma = pltpu.SemaphoreType.DMA
    far = pl.BlockSpec(memory_space=pltpu.HBM)
    pair = dma((cb,))
    return pl.pallas_call(
        functools.partial(kernel, (rb, cb, nb, proc_rows, nz)),
        out_shape=jax.ShapeDtypeStruct(matrix.shape, F32),
        in_specs=[far, far, far],
        out_specs=pl.BlockSpec(memory_space=pl.ANY),
        scratch_shapes=[
            pltpu.VMEM(pivots.shape, jnp.int32),
            pltpu.VMEM(inverse_blocks.shape, F32),
            pltpu.VMEM((cb, rows, nb), F32),
            pltpu.VMEM((3, rows, nb), BF16),
            pltpu.VMEM((cb, slots, nb), F32),
            pltpu.VMEM((cb, proc_rows, ch, nb), F32),
            pltpu.VMEM((cb, proc_rows, 2 * co, nb), F32),
            pltpu.VMEM((cb, proc_rows, ch, nb), F32),
            pltpu.VMEM((2, rows + nb, nb), F32),
            pltpu.VMEM((nb, nb), F32),
            pltpu.VMEM((cb, slots, nb), F32),
            pltpu.VMEM((3 * nb, nb), BF16),
            pltpu.VMEM((6 * nb, nb), BF16),
            pltpu.VMEM((6 * nb, cb * nb), BF16),
            pltpu.VMEM((3, slots, nb), BF16),
            dma((rb * cb + 2,)), dma((rb * cb,)),
            pair, pair, pair, dma((cb, 2)), pair, pair, pair, pair,
            dma, dma, dma((chunks,)), dma, dma((rb + 1,)),
        ],
        compiler_params=pltpu.CompilerParams(
            collective_id=0, has_side_effects=True, vmem_limit_bytes=50 * 2**20
        ),
    )(matrix, pivots, inverse_blocks)


def solution(mesh):
    spec = P(None, "prow", None, None, "pcol", None)
    return jax.shard_map(
        functools.partial(shards, mesh.shape["prow"], mesh.shape["pcol"]),
        mesh=mesh,
        in_specs=(spec, P(), P()),
        out_specs=spec,
        check_vma=False,
    )
```

```python
import functools

import jax
import jax.numpy as jnp
from jax import lax
from jax.experimental import pallas as pl
from jax.experimental.pallas import tpu as pltpu
from jax.sharding import PartitionSpec as P

F32, BF16 = jnp.float32, jnp.bfloat16
PIECE_OF_BLOCK = 8
EXTRA = 11


def mul(left, right):
    return jnp.dot(left, right, preferred_element_type=F32)


def parts2(x):
    high = x.astype(BF16)
    return high, (x - high.astype(F32)).astype(BF16)


def parts3(x):
    high = x.astype(BF16)
    rest = x - high.astype(F32)
    mid = rest.astype(BF16)
    return high, mid, (rest - mid.astype(F32)).astype(BF16)


def across(*x):
    return jnp.concatenate(x, axis=1)


def down(*x):
    return jnp.concatenate(x, axis=0)


def weights(x):
    high, low = parts2(x)
    return down(high, low, high)


def product(left, right):
    high, low = parts2(left)
    return mul(across(high, high, low), weights(right))


def kernel(
    sizes, x, piv_in, inv_in, out,
    piv, inv, a, split, picks, rs, aold, apr, panel, corner, u, w0, w1, wu, old,
    in_sem, out_sem, rs_send, rs_recv, old_send, old_recv, aold_send, aold_recv, apr_send, apr_recv,
    z_send, z_send2, z_recv, sib_send, sib_recv,
):
    rb, cb, nb, np_, nz = sizes
    rows, slots = rb * nb, 2 * nb
    ch, co = slots // np_, nb // np_
    half = np_ // 2
    piece = nb // PIECE_OF_BLOCK
    chunks = (rb + 1) * PIECE_OF_BLOCK
    early = (rb - 1) * PIECE_OF_BLOCK
    me = lax.axis_index("prow")
    col = lax.axis_index("pcol")
    z, core = col // 2, col % 2
    middle = nz // 2

    def at_row(r):
        return {"prow": r, "pcol": col}

    def at_col(zz, cc):
        return {"prow": me, "pcol": zz * 2 + cc}

    def loop(low, high, body):
        def step(d, carry):
            body(d)
            return carry

        lax.fori_loop(low, high, step, 0)

    def load(r, c):
        return pltpu.make_async_copy(
            x.at[r, 0, :, c, 0, :], a.at[c, pl.ds(r * nb, nb), :], in_sem.at[r * cb + c]
        )

    load_piv = pltpu.make_async_copy(piv_in, piv, in_sem.at[rb * cb])
    load_inv = pltpu.make_async_copy(inv_in, inv, in_sem.at[rb * cb + 1])
    load_piv.start()
    for c in range(cb):
        for r in range(rb):
            load(r, c).start()
    load_inv.start()

    children = [[] for _ in range(nz)]
    for sign, reach in ((1, middle), (-1, nz - middle - 1)):
        for n in range(1, reach + 1):
            parent = n - 2 if n % 2 == 0 else (n + 1 if n < reach else n - 1)
            children[sign * parent % nz].insert(0, sign * n % nz)
    partners = [children[zz] + [p for p in range(nz) if zz in children[p]] for zz in range(nz)]

    barrier = pltpu.get_barrier_semaphore()
    loop(1, np_, lambda d: pl.semaphore_signal(barrier, inc=1, device_id=at_row((me + d) % np_)))
    pl.semaphore_signal(barrier, inc=1, device_id=at_col(z, 1 - core))

    def with_partners(body):
        for zz in range(nz):
            @pl.when(z == zz)
            def _():
                body(partners[zz])

    def greet_line(others):
        for zz in others:
            pl.semaphore_signal(barrier, inc=1, device_id=at_col(zz, core))

    with_partners(greet_line)

    load_piv.wait()
    lane = lax.broadcasted_iota(jnp.int32, (nb, nb), 1)
    sub = lax.broadcasted_iota(jnp.int32, (nb, nb), 0)
    p0r, p1r = piv[0:1, :], piv[1:2, :]
    p0c = jnp.max(jnp.where(lane == sub, p0r, -1), axis=1, keepdims=True)
    p1c = jnp.max(jnp.where(lane == sub, p1r, -1), axis=1, keepdims=True)
    same = p1c == p0r
    back = jnp.max(jnp.where(same, lane, -1), axis=1, keepdims=True)
    src0, src1 = p0c, jnp.where(back >= 0, back, p1c)
    hit = jnp.max(jnp.where(p0r == sub + nb, p1c, -1), axis=0, keepdims=True)
    gone = jnp.max(jnp.where(same, 1, 0), axis=0, keepdims=True)
    dst0 = jnp.where(hit >= 0, hit, jnp.where(gone > 0, -1, p0r))
    up = jnp.max(jnp.where(p0c == lane + nb, 1, 0), axis=0, keepdims=True)
    dst1 = jnp.where(up > 0, -1, p1r)

    def old_copy(c, k, d):
        to = (me + d) % np_
        return pltpu.make_async_remote_copy(
            a.at[c, pl.ds(pl.multiple_of(to * co, co), co), :],
            aold.at[c, to, pl.ds(k * co, co), :],
            old_send.at[c], old_recv.at[c, k], device_id=at_row(to),
        )

    def old_scatter(c):
        for k in range(2):
            @pl.when(me == k)
            def _():
                loop(1, np_, lambda d: old_copy(c, k, d).start())
                aold[c, me, pl.ds(k * co, co), :] = a[c, pl.ds(pl.multiple_of(me * co, co), co), :]

    def old_ready(c):
        for k in range(2):
            @pl.when(me != k)
            def _():
                pltpu.make_async_remote_copy(
                    aold.at[c, me, pl.ds(k * co, co), :], aold.at[c, me, pl.ds(k * co, co), :],
                    old_send.at[c], old_recv.at[c, k], device_id=at_row((me + 1) % np_),
                ).wait_recv()

    def old_drain(c):
        for k in range(2):
            @pl.when(me == k)
            def _():
                sent = a.at[c, pl.ds(0, nb - co), :]
                pltpu.make_async_remote_copy(
                    sent, sent, old_send.at[c], old_recv.at[c, k], device_id=at_row((me + 1) % np_)
                ).wait_send()

    def gather(buf, send, recv, c):
        def start(d):
            pltpu.make_async_remote_copy(
                buf.at[c, me], buf.at[c, me], send.at[c], recv.at[c], device_id=at_row((me + d) % np_)
            ).start()

        loop(1, np_, start)

    def peers(buf, send, recv, c):
        others = buf.at[c, pl.ds(0, np_ - 1)]
        return pltpu.make_async_remote_copy(
            others, others, send.at[c], recv.at[c], device_id=at_row((me + 1) % np_)
        )

    def gather_wait(*which):
        peers(*which).wait_recv()

    old_g, pr_g = (aold, aold_send, aold_recv), (apr, apr_send, apr_recv)

    def pick(c):
        def step(r):
            h, m, l = parts3(a[c, pl.ds(pl.multiple_of(r * nb, nb), nb), :])
            split[0, pl.ds(pl.multiple_of(r * nb, nb), nb), :] = h
            split[1, pl.ds(pl.multiple_of(r * nb, nb), nb), :] = m
            split[2, pl.ds(pl.multiple_of(r * nb, nb), nb), :] = l

        loop(0, rb, step)
        for k, src in ((0, src0), (1, src1)):
            chosen = across(*[(src == (r * np_ + me) * nb + lane).astype(F32).astype(BF16) for r in range(rb)])
            picks[c, pl.ds(k * nb, nb), :] = mul(chosen, split[0]) + mul(chosen, split[1]) + mul(chosen, split[2])

    def rs_start(c):
        rs[c, me] = picks[c, pl.ds(pl.multiple_of(me * ch, ch), ch), :]

        def start(d):
            to = (me + d) % np_
            pltpu.make_async_remote_copy(
                picks.at[c, pl.ds(pl.multiple_of(to * ch, ch), ch), :], rs.at[c, me],
                rs_send.at[c], rs_recv.at[c], device_id=at_row(to),
            ).start()

        loop(1, np_, start)

    def rs_finish(c):
        peers(rs, rs_send, rs_recv, c).wait_recv()
        apr[c, me] = jnp.sum(rs[c], axis=0)

    def old_parts(c):
        for k in range(2):
            at = pl.ds(k * nb, nb)
            old[0, at, :], old[1, at, :], old[2, at, :] = parts3(aold[c, :, pl.ds(k * co, co), :].reshape(nb, nb))

    def place(c, r):
        at = pl.ds(r * nb, nb)
        here = (r * np_ + me) * nb + sub
        put0, put1 = (dst0 == here).astype(F32), (dst1 == here).astype(F32)
        moved = jnp.max(jnp.maximum(put0, put1), axis=1, keepdims=True)
        put = across(put0.astype(BF16), put1.astype(BF16))
        total = mul(put, old[0]) + mul(put, old[1]) + mul(put, old[2])
        a[c, at, :] = jnp.where(moved > 0, total, a[c, at, :])

    def piece_at(i, which):
        return panel.at[which, pl.ds(pl.multiple_of(i * piece, piece), piece), :]

    def z_copy(i, zz, sem):
        at = piece_at(i, core)
        return pltpu.make_async_remote_copy(at, at, sem, z_recv.at[i], device_id=at_col(zz, core))

    def sib_copy(i):
        at = piece_at(i, core)
        return pltpu.make_async_remote_copy(
            at, at, sib_send, sib_recv.at[i // PIECE_OF_BLOCK], device_id=at_col(z, 1 - core)
        )

    def sib_wait(t):
        at = panel.at[1 - core, pl.ds(t * nb, nb), :]
        pltpu.make_async_remote_copy(at, at, sib_send, sib_recv.at[t], device_id=at_col(z, 1 - core)).wait_recv()

    def pass_on(i):
        for zz in range(nz):
            if children[zz]:
                @pl.when(z == zz)
                def _():
                    for child, sem in zip(children[zz], (z_send, z_send2)):
                        z_copy(i, child, sem).start()

    def send(i):
        pass_on(i)
        sib_copy(i).start()

    def relay(i):
        z_copy(i, z, z_send).wait_recv()
        pass_on(i)
        sib_copy(i).start()

    def tile(r):
        return pl.ds((r if r < rb - 1 else rb) * nb, nb)

    solved = pl.ds((rb - 1) * nb, nb)

    def chosen_rows(c, k):
        return apr[c, pl.ds(k * half, half), :, :].reshape(nb, nb)

    def block(c):
        return col if c == 0 else c * 2 * nz + col

    def upper(k):
        return jnp.where(lane >= sub, inv[k], 0.0)

    def lower(k):
        return jnp.where(lane < sub, inv[k], 0.0) + jnp.where(lane == sub, 1.0, 0.0)

    def solve_first():
        w0[...] = weights(upper(0))
        for c in range(cb):
            u[c, pl.ds(0, nb), :] = jnp.where(block(c) > 0, product(lower(0), chosen_rows(c, 0)), 0.0)

    def solve_corner():
        sib_wait(rb - 1)
        corner[...] = product(panel[0, solved, :], upper(0))
        u01 = product(lower(0), panel[1, solved, :])
        cross = product(product(upper(0), u01), upper(1))
        w1[...] = weights(down(-cross, upper(1)))

    def solve_second():
        for c in range(cb):
            left = chosen_rows(c, 1) - product(corner[...], u[c, pl.ds(0, nb), :])
            u[c, pl.ds(nb, nb), :] = jnp.where(block(c) > 1, product(lower(1), left), 0.0)
            wu[:, pl.ds(c * nb, nb)] = weights(u[c])

    def store(r, c):
        return pltpu.make_async_copy(
            a.at[c, pl.ds(r * nb, nb), :], out.at[r, 0, :, c, 0, :], out_sem.at[r * cb + c]
        )

    def update(r):
        sib_wait(r if r < rb - 1 else rb)
        at = pl.ds(r * nb, nb)
        part = r * np_ + me
        c0h, c0l = parts2(panel[0, tile(r), :])
        c1h, c1l = parts2(panel[1, tile(r), :])
        l0 = mul(across(c0h, c0h, c0l), w0[...])
        l1 = mul(across(c0h, c1h, c0h, c1h, c0l, c1l), w1[...])
        if r == 0:
            l0 = jnp.where(me == 0, 0.0, jnp.where(me == 1, corner[...], l0))
            l1 = jnp.where(me <= 1, 0.0, l1)
        high, low = parts2(across(l0, l1))
        change = mul(across(high, high, low), wu[...])
        for c in range(cb):
            total = a[c, at, :]
            if r == 0:
                total = jnp.where(me == 0, chosen_rows(c, 0), jnp.where(me == 1, chosen_rows(c, 1), total))
            total = total - change[:, c * nb : (c + 1) * nb]
            if r == 0:
                for k in range(2):
                    mine = jnp.logical_and(part == k, block(c) > k)
                    total = jnp.where(mine, u[c, pl.ds(k * nb, nb), :], total)
            if c == 0:
                for k, l in enumerate((l0, l1)):
                    total = jnp.where(jnp.logical_and(col == k, part > k), l, total)
            a[c, at, :] = total
            store(r, c).start()

    load(0, 0).wait()
    with_partners(lambda others: pl.semaphore_wait(barrier, np_ + len(others)))
    old_scatter(0)
    for r in range(1, rb):
        load(r, 0).wait()
    pick(0)
    old_ready(0)
    gather(*old_g, 0)
    rs_start(0)
    for c in range(1, cb):
        for r in range(rb):
            load(r, c).wait()
        old_scatter(c)
    load_inv.wait()

    @pl.when(z == 0)
    def _():
        gather_wait(*old_g, 0)
        old_drain(0)
        old_parts(0)
        for r in range(rb):
            place(0, r)
            panel[core, tile(r), :] = a[0, pl.ds(r * nb, nb), :]
            if r < rb - 1:
                loop(r * PIECE_OF_BLOCK, (r + 1) * PIECE_OF_BLOCK, send)
        rs_finish(0)
        gather(*pr_g, 0)
        for c in range(1, cb):
            pick(c)
            old_ready(c)
        gather_wait(*pr_g, 0)
        for k in range(2):
            @pl.when(core == k)
            def _():
                panel[core, solved, :] = chosen_rows(0, 1 - k)
        loop(early, chunks, send)
        for c in range(1, cb):
            rs_start(c)
            gather(*old_g, c)
            rs_finish(c)
            gather(*pr_g, c)

    @pl.when(z != 0)
    def _():
        for c in range(1, cb):
            pick(c)
            rs_start(c)
            old_ready(c)
            gather(*old_g, c)

    def place_all(c):
        gather_wait(*old_g, c)
        old_drain(c)
        old_parts(c)
        for r in range(rb):
            place(c, r)

    def first_column():
        @pl.when(z != 0)
        def _():
            place_all(0)

    def second_column():
        for c in range(1, cb):
            place_all(c)

    def rows_here():
        @pl.when(z != 0)
        def _():
            gather_wait(*pr_g, 0)

        for c in range(1, cb):
            gather_wait(*pr_g, c)
        solve_first()

    def early_tiles():
        for r in range(rb - 1):
            update(r)

    near = jnp.where(z > middle, nz - z, z)
    turn = jnp.where(near < 5, 14 - 3 * near, 0)
    begin = 33 - 3 * near
    finish = jnp.where(near < middle - 1, chunks, early + PIECE_OF_BLOCK + 1)
    finish = jnp.where(begin + 15 > finish, begin + 15, finish)
    jobs = (
        (begin, first_column), (begin + 3, second_column), (begin + 14, rows_here),
        (finish, solve_corner), (finish + 1, solve_second), (finish + 2, early_tiles),
    )

    def step(i):
        @pl.when(jnp.logical_and(z != 0, i == turn))
        def _():
            for c in range(cb):
                rs_finish(c)
                gather(*pr_g, c)

        @pl.when(jnp.logical_and(z != 0, i < chunks))
        def _():
            relay(i)

        for when, job in jobs:
            pl.when(i == when)(job)

    loop(0, chunks + EXTRA, step)
    update(rb - 1)

    for c in range(cb):
        peers(rs, rs_send, rs_recv, c).wait_send()
        peers(*old_g, c).wait_send()
        peers(*pr_g, c).wait_send()
    whole = panel.at[core]

    def sent(sem):
        pltpu.make_async_remote_copy(whole, whole, sem, z_recv.at[0], device_id=at_col(z, 1 - core)).wait_send()

    sent(sib_send)

    for zz in range(nz):
        if children[zz]:
            @pl.when(z == zz)
            def _():
                for _, sem in zip(children[zz], (z_send, z_send2)):
                    sent(sem)

    for r in range(rb):
        for c in range(cb):
            store(r, c).wait()


def shards(proc_rows, proc_cols, matrix, pivots, inverse_blocks):
    rb, _, nb, cb, _, _ = matrix.shape
    nz = proc_cols // 2
    rows, slots = rb * nb, 2 * nb
    ch, co = slots // proc_rows, nb // proc_rows
    chunks = (rb + 1) * PIECE_OF_BLOCK
    dma = pltpu.SemaphoreType.DMA
    far = pl.BlockSpec(memory_space=pltpu.HBM)
    pair = dma((cb,))
    return pl.pallas_call(
        functools.partial(kernel, (rb, cb, nb, proc_rows, nz)),
        out_shape=jax.ShapeDtypeStruct(matrix.shape, F32),
        in_specs=[far, far, far],
        out_specs=pl.BlockSpec(memory_space=pl.ANY),
        scratch_shapes=[
            pltpu.VMEM(pivots.shape, jnp.int32),
            pltpu.VMEM(inverse_blocks.shape, F32),
            pltpu.VMEM((cb, rows, nb), F32),
            pltpu.VMEM((3, rows, nb), BF16),
            pltpu.VMEM((cb, slots, nb), F32),
            pltpu.VMEM((cb, proc_rows, ch, nb), F32),
            pltpu.VMEM((cb, proc_rows, 2 * co, nb), F32),
            pltpu.VMEM((cb, proc_rows, ch, nb), F32),
            pltpu.VMEM((2, rows + nb, nb), F32),
            pltpu.VMEM((nb, nb), F32),
            pltpu.VMEM((cb, slots, nb), F32),
            pltpu.VMEM((3 * nb, nb), BF16),
            pltpu.VMEM((6 * nb, nb), BF16),
            pltpu.VMEM((6 * nb, cb * nb), BF16),
            pltpu.VMEM((3, slots, nb), BF16),
            dma((rb * cb + 2,)), dma((rb * cb,)),
            pair, pair, pair, dma((cb, 2)), pair, pair, pair, pair,
            dma, dma, dma((chunks,)), dma, dma((rb + 1,)),
        ],
        compiler_params=pltpu.CompilerParams(
            collective_id=0, has_side_effects=True, vmem_limit_bytes=50 * 2**20
        ),
    )(matrix, pivots, inverse_blocks)


def solution(mesh):
    spec = P(None, "prow", None, None, "pcol", None)
    return jax.shard_map(
        functools.partial(shards, mesh.shape["prow"], mesh.shape["pcol"]),
        mesh=mesh,
        in_specs=(spec, P(), P()),
        out_specs=spec,
        check_vma=False,
    )
```
